128 devices in a mesh: ctx: 32 (over z, y_hi, x), dp: 4 (over y_lo, core).
Axes of the slice: x: 4, y: 4 (y_hi: 2, y_lo: 2; y = y_hi * 2 + y_lo), z: 4, core: 2. Of those that a mesh axis runs over, the one named last changes fastest.
Arguments:
- queries: bfloat16 [32768, 1024], P(('dp', 'ctx')), parts along dimension 0, may hold values from -6 to 6
- keys: bfloat16 [32768, 128], P(('dp', 'ctx')), parts along dimension 0, may hold values from -6 to 6
- values: bfloat16 [32768, 128], P(('dp', 'ctx')), parts along dimension 0, may hold values from -6 to 6
- outputs: bfloat16 [32768, 1024], P(('dp', 'ctx')), parts along dimension 0, may hold values from -6 to 6
- out_grad: bfloat16 [32768, 1024], P(('dp', 'ctx')), parts along dimension 0, may hold values from -6 to 6
- lse: float32 [8, 32768], P(None, ('dp', 'ctx')), parts along dimension 1, as said below
- block_order: int32 [256], P('dp'), parts along dimension 0, may hold values from 0 to 63, as said below
- doc_lengths: int32 [64], P('dp'), parts along dimension 0, may hold values from 1 to 4096, as said below
Outputs:
- query_grad: bfloat16 [32768, 1024], P(('dp', 'ctx')), parts along dimension 0
- key_grad: bfloat16 [32768, 128], P(('dp', 'ctx')), parts along dimension 0
- value_grad: bfloat16 [32768, 128], P(('dp', 'ctx')), parts along dimension 0
The draws below stay inside these ranges and needn't reach their ends.
There are 4 independent parts, one for each index of `dp`. The reference program is written for one: setup_inputs(seed, part) draws one part's arguments, and reference() takes and returns one part's arrays. A program takes and returns all parts, laid end to end along the dimension named above; each array names one. Nothing has to cross between parts.
Inputs may be any that keep to these rules, and one draw needn't show every extreme that they name: `block_order`: A permutation of the 64 sequence blocks. `doc_lengths`: positive lengths summing to 8192; the longest document has exactly 4096 tokens. `lse`: each entry exceeds the logarithm of the number of keys that its query may attend to.
All inputs are finite; a program needn't handle non-finite values.
Results may differ from the reference program's by a relative error of at most 0.0052.
Values may be sent and summed in bfloat16 or wider, within the bound.
A program may use at most 64 MiB of HBM per device.

```python
import jax
import jax.numpy as jnp
from jax import lax

HEADS = 8
HD = 128
TOK_DEV = 256
DOCS = 16
BLOCK = 128
SEQ = 8192
BLOCKS = 64
MOST = 4096
N_CTX = 32


def order_helper(key):
    return jax.random.permutation(jax.random.fold_in(key, 11), BLOCKS).astype(jnp.int32)


def lengths_helper(key):
    key = jax.random.fold_in(key, 12)
    remain = SEQ - MOST
    picks = jax.random.permutation(jax.random.fold_in(key, 1), remain - 1)[:DOCS - 2] + 1
    cuts = jnp.sort(picks.astype(jnp.int32))
    bounds = jnp.concatenate([jnp.zeros((1,), jnp.int32), cuts, jnp.full((1,), remain, jnp.int32)])
    pieces = bounds[1:] - bounds[:-1]
    whole = jnp.concatenate([jnp.full((1,), MOST, jnp.int32), pieces])
    return jax.random.permutation(jax.random.fold_in(key, 2), whole).astype(jnp.int32)


def draw_block_order(key, part):
    return order_helper(key)


def draw_doc_lengths(key, part):
    return lengths_helper(key)


def draw_lse(key, part):
    order = order_helper(key)
    lengths = lengths_helper(key)
    key = jax.random.fold_in(key, 3)
    rows = jnp.arange(SEQ, dtype=jnp.int32)
    places = order[rows // BLOCK] * BLOCK + rows % BLOCK
    ends = jnp.cumsum(lengths)
    begins = jnp.sum(jnp.where(ends[None, :] <= places[:, None], lengths[None, :], 0), axis=1)
    count = (places - begins + 1).astype(jnp.float32)
    extra = jax.random.uniform(key, (HEADS, SEQ), jnp.float32, 0.3, 1.2)
    return (jnp.log(count)[None, :] + extra).astype(jnp.float32)


def levels(stream_key, shape, cuts, low, high):
    def one(axis_at, shards_of):
        steps = jax.random.uniform(jax.random.fold_in(jax.random.fold_in(stream_key, 6), axis_at), (shards_of,), jnp.float32, low / len(cuts), high / len(cuts))
        return jnp.repeat(jnp.exp(steps), shape[axis_at] // shards_of).reshape((-1,) + (1,) * (len(shape) - axis_at - 1))

    gain = one(*cuts[0])
    for cut in cuts[1:]:
        gain = gain * one(*cut)
    return gain


def gaussian(rng, shape, width, reach, cuts=(), held_as=jnp.bfloat16):
    drawn = width * jax.random.normal(rng, shape, jnp.float32)
    if cuts:
        drawn = drawn * levels(rng, shape, cuts, -0.22, 0.18)
    return jnp.clip(drawn, -reach, reach).astype(held_as)


def setup_inputs(seed: int = 0, part: int = 0) -> dict:
    streams_of = jax.random.split(jax.random.key(seed), 9)
    own_keys = jax.random.split(jax.random.fold_in(streams_of[8], part), 9)
    return {
        "queries": gaussian(own_keys[0], (SEQ, HEADS * HD), 1.0, 6.0, ((0, 32),)),
        "keys": gaussian(own_keys[1], (SEQ, HD), 1.0, 6.0, ((0, 32),)),
        "values": gaussian(own_keys[2], (SEQ, HD), 1.0, 6.0, ((0, 32),)),
        "outputs": gaussian(own_keys[3], (SEQ, HEADS * HD), 1.0, 6.0, ((0, 32),)),
        "out_grad": gaussian(own_keys[4], (SEQ, HEADS * HD), 1.0, 6.0, ((0, 32),)),
        "lse": draw_lse(jax.random.fold_in(jax.random.fold_in(streams_of[8], part), 71), part),
        "block_order": draw_block_order(jax.random.fold_in(jax.random.fold_in(streams_of[8], part), 71), part),
        "doc_lengths": draw_doc_lengths(jax.random.fold_in(jax.random.fold_in(streams_of[8], part), 71), part),
    }


def positions(block_order, rows):
    return block_order[rows // BLOCK] * BLOCK + rows % BLOCK


def documents(doc_lengths, places):
    ends = jnp.cumsum(doc_lengths)
    return jnp.sum((ends[None, :] <= places[:, None]).astype(jnp.int32), axis=1)


def reference(queries, keys, values, outputs, out_grad, lse, block_order, doc_lengths):
    scale = HD ** -0.5
    places = positions(block_order, jnp.arange(SEQ, dtype=jnp.int32))
    docs = documents(doc_lengths, places)

    def visit(carry, index):
        key_acc, value_acc = carry
        start = (index * TOK_DEV).astype(jnp.int32)
        query_rows = lax.dynamic_slice_in_dim(queries, start, TOK_DEV, 0).reshape(TOK_DEV * HEADS, HD)
        grad_rows = lax.dynamic_slice_in_dim(out_grad, start, TOK_DEV, 0)
        out_rows = lax.dynamic_slice_in_dim(outputs, start, TOK_DEV, 0)
        stats = lax.dynamic_slice_in_dim(lse, start, TOK_DEV, 1).T.reshape(-1)
        delta = jnp.sum((grad_rows.astype(jnp.float32) * out_rows.astype(jnp.float32)).reshape(TOK_DEV, HEADS, HD), axis=2).reshape(-1)
        grad_rows = grad_rows.reshape(TOK_DEV * HEADS, HD)
        query_pos = jnp.repeat(lax.dynamic_slice_in_dim(places, start, TOK_DEV, 0), HEADS)
        query_doc = jnp.repeat(lax.dynamic_slice_in_dim(docs, start, TOK_DEV, 0), HEADS)
        allowed = (places[None, :] <= query_pos[:, None]) & (docs[None, :] == query_doc[:, None])
        score = scale * jnp.dot(query_rows, keys.T, preferred_element_type=jnp.float32)
        prob = jnp.where(allowed, jnp.exp(score - stats[:, None]), jnp.float32(0.0))
        prob_b = prob.astype(jnp.bfloat16)
        dprob = jnp.dot(grad_rows, values.T, preferred_element_type=jnp.float32)
        dscore = (prob * (dprob - delta[:, None])).astype(jnp.bfloat16)
        query_part = (scale * jnp.dot(dscore, keys, preferred_element_type=jnp.float32)).astype(jnp.bfloat16)
        key_acc = key_acc + jnp.dot(dscore.T, query_rows, preferred_element_type=jnp.float32)
        value_acc = value_acc + jnp.dot(prob_b.T, grad_rows, preferred_element_type=jnp.float32)
        return (key_acc, value_acc), query_part.reshape(TOK_DEV, HEADS * HD)

    empty = jnp.zeros((SEQ, HD), jnp.float32)
    (key_acc, value_acc), query_parts = lax.scan(visit, (empty, empty), jnp.arange(N_CTX, dtype=jnp.int32))
    query_grad = query_parts.reshape(SEQ, HEADS * HD)
    key_grad = (scale * key_acc).astype(jnp.bfloat16)
    value_grad = value_acc.astype(jnp.bfloat16)
    return (query_grad, key_grad, value_grad)
```

```python
import functools

import jax
import jax.numpy as jnp
from jax import lax
from jax.experimental import pallas as pl
from jax.experimental.pallas import tpu as pltpu
from jax.sharding import PartitionSpec as P

BF = jnp.bfloat16
F32 = jnp.float32
I32 = jnp.int32
MESH = pl.DeviceIdType.MESH
VM = pl.BlockSpec(memory_space=pltpu.VMEM)
SM = pl.BlockSpec(memory_space=pltpu.SMEM)

RING = 4
PLANE = RING * RING
T = 256
B = 128
H = 8
D = 128
VMEM_LIMIT = 56 * 2**20


def dot(a, b, ca, cb):
    return lax.dot_general(a, b, (((ca,), (cb,)), ((), ())), preferred_element_type=F32)


def coords():
    me = lax.axis_index("ctx")
    return me // 8, (me // 4) % 2, me % 4


def ident(z, y, x):
    return {"ctx": z * 8 + y * 4 + x}


def step_of(v, d):
    return lax.rem(v + d, RING)


def greet(z, y, x, pair):
    barrier = pltpu.get_barrier_semaphore()
    others = [ident(z, y, step_of(x, d)) for d in (1, 2, 3)]
    others += [ident(step_of(z, d), y, x) for d in (1, 2, 3)]
    if pair:
        others.append(ident(z, 1 - y, x))
    for other in others:
        pl.semaphore_signal(barrier, inc=1, device_id=other, device_id_type=MESH)
    pl.semaphore_wait(barrier, len(others))


def gather_kernel(
    k_ref, v_ref, g_ref, o_ref, lse_ref, ka, va, delta, pair_delta, pair_lse,
    own_sem, s1, r1, s2, r2, ps, pr,
):
    z, y, x = coords()
    greet(z, y, x, True)
    here = z * RING + x
    pair = ident(z, 1 - y, x)

    def send(src, dst, ssem, rsem, to):
        copy = pltpu.make_async_remote_copy(
            src_ref=src, dst_ref=dst, send_sem=ssem, recv_sem=rsem, device_id=to, device_id_type=MESH
        )
        copy.start()
        return copy

    srcs, alls = (k_ref, v_ref), (ka, va)

    def first_peer(a, d):
        return ident(z, y, step_of(x, d)) if a == 0 else ident(step_of(z, d), y, x)

    def second_peer(a, d):
        return first_peer(1 - a, d)

    def slot_from(a, s):
        return z * RING + step_of(x, RING - s) if a == 0 else step_of(z, RING - s) * RING + x

    first, second = {}, {}
    for a in (0, 1):
        for d in (1, 3, 2):
            first[a, d] = send(srcs[a], alls[a].at[here], s1.at[a, d - 1], r1.at[a, d - 1], first_peer(a, d))
    for a in (0, 1):
        for d in (1, 3, 2):
            second[a, 0, d] = send(srcs[a], alls[a].at[here], s2.at[a, 0, d - 1], r2.at[a, 0, d - 1], second_peer(a, d))
    own = []
    for a in (0, 1):
        copy = pltpu.make_async_copy(srcs[a], alls[a].at[here], own_sem.at[a])
        copy.start()
        own.append(copy)
    lse_copy = send(lse_ref, pair_lse, ps.at[0], pr.at[0], pair)

    ones = jnp.ones((8, D), BF)
    for h in range(H):
        cols = slice(h * D, (h + 1) * D)
        prod = g_ref[:, cols].astype(F32) * o_ref[:, cols].astype(F32)
        hi = prod.astype(BF)
        lo = (prod - hi.astype(F32)).astype(BF)
        total = dot(ones, hi, 1, 1) + dot(ones, lo, 1, 1)
        delta[h : h + 1, :] = total[0:1, :]
    delta_copy = send(delta, pair_delta, ps.at[1], pr.at[1], pair)

    for s in (1, 3, 2):
        for a in (0, 1):
            first[a, s].wait_recv()
            block = alls[a].at[slot_from(a, s)]
            for d in (1, 3, 2):
                second[a, s, d] = send(block, block, s2.at[a, s, d - 1], r2.at[a, s, d - 1], second_peer(a, d))
    for copy in own:
        copy.wait()
    for copy in second.values():
        copy.wait_recv()
    for copy in (lse_copy, delta_copy):
        copy.wait()
    for copy in list(first.values()) + list(second.values()):
        copy.wait_send()


def gather(keys, values, out_grad, outputs, lse):
    return pl.pallas_call(
        gather_kernel,
        out_shape=(
            jax.ShapeDtypeStruct((PLANE, T, D), BF),
            jax.ShapeDtypeStruct((PLANE, T, D), BF),
            jax.ShapeDtypeStruct((H, T), F32),
            jax.ShapeDtypeStruct((H, T), F32),
            jax.ShapeDtypeStruct((H, T), F32),
        ),
        in_specs=[VM] * 5,
        out_specs=(VM,) * 5,
        scratch_shapes=[
            pltpu.SemaphoreType.DMA((2,)),
            pltpu.SemaphoreType.DMA((2, 3)),
            pltpu.SemaphoreType.DMA((2, 3)),
            pltpu.SemaphoreType.DMA((2, 4, 3)),
            pltpu.SemaphoreType.DMA((2, 4, 3)),
            pltpu.SemaphoreType.DMA((2,)),
            pltpu.SemaphoreType.DMA((2,)),
        ],
        compiler_params=pltpu.CompilerParams(
            collective_id=0, has_side_effects=True, vmem_limit_bytes=VMEM_LIMIT
        ),
        name="gather_kv",
    )(keys, values, out_grad, outputs, lse)


def attend_kernel(
    start, who, order, lens, q_ref, g_ref, lse_ref, delta_ref, k_ref, v_ref, *rest
):
    if start:
        dq_ref, dk, dv = rest[:3]
        scratch = rest[3:]
        dk[...] = jnp.zeros_like(dk)
        dv[...] = jnp.zeros_like(dv)
    else:
        dk_in, dv_in, dq_ref, dk_out, dv_out = rest[:5]
        scratch = rest[5:]
        dk, dv = dk_in, dv_in
    inv, ends, item_q, item_a, item_b, pos_a, pos_b, qr, gr, lr, dr, qpos, qfrom, dqa, pbuf, dbuf = scratch
    owner, plane = who[0], who[1]

    def invert(s, c):
        inv[order[s]] = s
        return c

    lax.fori_loop(0, 64, invert, 0)

    def add_end(d, c):
        c = c + lens[d]
        ends[d] = c
        return c

    lax.fori_loop(0, 16, add_end, jnp.int32(0))
    lane = lax.broadcasted_iota(I32, (1, 2 * B), 1) % B

    count = jnp.int32(0)
    for blk in (0, 1):
        at = order[owner * 2 + blk]
        base = at * B
        places = base + lane
        begin = jnp.zeros_like(places)
        low = jnp.int32(0)
        for d in range(16):
            begin = jnp.where(ends[d] <= places, ends[d], begin)
            low = jnp.where(ends[d] <= base, ends[d], low)
        qpos[blk] = places
        qfrom[blk] = begin

        def visit(p, c):
            n, half = c
            s = inv[p]
            dev = s // 2
            mine = (dev // 4) % 2 == plane
            slot = ((dev // 8) * RING + dev % 4) * 2 + s % 2

            @pl.when(mine & (half == 0))
            def _():
                item_q[n] = blk
                item_a[n] = slot
                pos_a[n] = p * B
                item_b[n] = 0
                pos_b[n] = 1 << 20

            @pl.when(mine & (half == 1))
            def _():
                item_b[n] = slot
                pos_b[n] = p * B

            full = mine & (half == 1)
            return jnp.where(full, n + 1, n), jnp.where(mine, 1 - half, half)

        n, half = lax.fori_loop(low // B, at + 1, visit, (count, jnp.int32(0)))
        count = n + half

    item_q[count] = 0
    item_a[count] = 0
    item_b[count] = 0
    pos_a[count] = 1 << 20
    pos_b[count] = 1 << 20

    for blk in (0, 1):
        rows = slice(blk * B, (blk + 1) * B)
        for h in range(H):
            cols = slice(h * D, (h + 1) * D)
            qr[blk, cols, :] = q_ref[rows, cols]
            gr[blk, cols, :] = g_ref[rows, cols]
            lr[blk, :, cols] = lse_ref[h : h + 1, rows]
            dr[blk, :, cols] = delta_ref[h : h + 1, rows]
    dqa[...] = jnp.zeros_like(dqa)
    scale = jnp.float32(D**-0.5)
    down = lax.broadcasted_iota(I32, (B, 2 * B), 0)

    def one(n, par):
        blk, a, b = item_q[n], item_a[n], item_b[n]
        kk = jnp.concatenate([k_ref[a], k_ref[b]], axis=0)
        vv = jnp.concatenate([v_ref[a], v_ref[b]], axis=0)
        key_pos = jnp.concatenate([pos_a[n] + down, pos_b[n] + down], axis=0)
        allowed = (key_pos <= qpos[blk]) & (key_pos >= qfrom[blk])
        for half in range(4):
            cols = slice(half * 256, (half + 1) * 256)
            score = dot(kk, qr[blk, cols, :], 1, 1)
            dprob = dot(vv, gr[blk, cols, :], 1, 1)
            prob = jnp.where(allowed, jnp.exp(score * scale - lr[blk, :, cols]), 0.0)
            pbuf[par, :, cols] = prob.astype(BF)
            dbuf[par, :, cols] = (prob * (dprob - dr[blk, :, cols])).astype(BF)
        dqa[blk] += dot(kk, dbuf[par], 0, 0)
        dv_term = jnp.dot(pbuf[par], gr[blk], preferred_element_type=F32)
        dk_term = jnp.dot(dbuf[par], qr[blk], preferred_element_type=F32)
        dk[a] += dk_term[:B]
        dk[b] += dk_term[B:]
        dv[a] += dv_term[:B]
        dv[b] += dv_term[B:]

    def two(i, c):
        one(2 * i, 0)
        one(2 * i + 1, 1)
        return c

    lax.fori_loop(0, (count + 1) // 2, two, 0)

    for blk in (0, 1):
        for h in range(H):
            cols = slice(h * D, (h + 1) * D)
            dq_ref[blk * B : (blk + 1) * B, cols] = dqa[blk, :, cols].T.astype(dq_ref.dtype)
    if not start:
        dk_out[...] = dk[...].astype(BF)
        dv_out[...] = dv[...].astype(BF)


def attend(who, order, lens, q, g, lse, delta, k, v, sums=None):
    start = sums is None
    kind = F32 if start else BF
    grads = jax.ShapeDtypeStruct((2 * PLANE, B, D), kind)
    args = [who, order, lens, q, g, lse, delta, k, v] + ([] if start else list(sums))
    return pl.pallas_call(
        functools.partial(attend_kernel, start),
        out_shape=(jax.ShapeDtypeStruct((T, H * D), kind), grads, grads),
        in_specs=[SM] * 3 + [VM] * (len(args) - 3),
        out_specs=(VM,) * 3,
        scratch_shapes=[
            pltpu.SMEM((64,), I32),
            pltpu.SMEM((16,), I32),
            pltpu.SMEM((72,), I32),
            pltpu.SMEM((72,), I32),
            pltpu.SMEM((72,), I32),
            pltpu.SMEM((72,), I32),
            pltpu.SMEM((72,), I32),
            pltpu.VMEM((2, H * B, D), BF),
            pltpu.VMEM((2, H * B, D), BF),
            pltpu.VMEM((2, 1, H * B), F32),
            pltpu.VMEM((2, 1, H * B), F32),
            pltpu.VMEM((2, 1, 2 * B), I32),
            pltpu.VMEM((2, 1, 2 * B), I32),
            pltpu.VMEM((2, D, H * B), F32),
            pltpu.VMEM((2, 2 * B, H * B), BF),
            pltpu.VMEM((2, 2 * B, H * B), BF),
        ],
        compiler_params=pltpu.CompilerParams(vmem_limit_bytes=VMEM_LIMIT),
        name="attend_own" if start else "attend_pair",
    )(*args)


def reduce_kernel(dk_ref, dv_ref, key_ref, value_ref, in1, out2, in2, s1, r1, s2, r2):
    z, y, x = coords()
    greet(z, y, x, False)
    srcs = (dk_ref, dv_ref)

    def send(src, dst, ssem, rsem, to):
        copy = pltpu.make_async_remote_copy(
            src_ref=src, dst_ref=dst, send_sem=ssem, recv_sem=rsem, device_id=to, device_id_type=MESH
        )
        copy.start()
        return copy

    def first_peer(a, d):
        return ident(step_of(z, d), y, x) if a == 0 else ident(z, y, step_of(x, d))

    def second_peer(a, e):
        return first_peer(1 - a, e)

    def slot(a, d, e):
        if a == 0:
            return step_of(z, d) * RING + step_of(x, e)
        return step_of(z, e) * RING + step_of(x, d)

    first, second = {}, {}
    for e in (2, 1, 3, 0):
        for a in (0, 1):
            for d in (2, 1, 3):
                first[a, e, d] = send(
                    srcs[a].at[slot(a, d, e)], in1.at[a, e, d - 1], s1.at[a, e, d - 1], r1.at[a, e, d - 1],
                    first_peer(a, d),
                )
    outs, scales = (key_ref, value_ref), (jnp.float32(D**-0.5), jnp.float32(1.0))
    sums = []
    for e in (2, 1, 3, 0):
        for a in (0, 1):
            total = srcs[a][slot(a, 0, e)].astype(F32)
            for d in (1, 2, 3):
                first[a, e, d].wait_recv()
                total = total + in1[a, e, d - 1].astype(F32)
            if e:
                out2[a, e - 1] = total.astype(BF)
                second[a, e] = send(out2.at[a, e - 1], in2.at[a, e - 1], s2.at[a, e - 1], r2.at[a, e - 1], second_peer(a, e))
            else:
                sums.append(total)
    for a in (0, 1):
        total = sums[a]
        for e in (1, 2, 3):
            second[a, e].wait_recv()
            total = total + in2[a, e - 1].astype(F32)
        outs[a][...] = (total * scales[a]).astype(BF)
    for copy in list(first.values()) + list(second.values()):
        copy.wait_send()


def reduce(dk, dv):
    grad = jax.ShapeDtypeStruct((T, D), BF)
    return pl.pallas_call(
        reduce_kernel,
        out_shape=(grad, grad),
        in_specs=[VM] * 2,
        out_specs=(VM,) * 2,
        scratch_shapes=[
            pltpu.VMEM((2, 4, 3, T, D), BF),
            pltpu.VMEM((2, 3, T, D), BF),
            pltpu.VMEM((2, 3, T, D), BF),
            pltpu.SemaphoreType.DMA((2, 4, 3)),
            pltpu.SemaphoreType.DMA((2, 4, 3)),
            pltpu.SemaphoreType.DMA((2, 3)),
            pltpu.SemaphoreType.DMA((2, 3)),
        ],
        compiler_params=pltpu.CompilerParams(
            collective_id=1, has_side_effects=True, vmem_limit_bytes=VMEM_LIMIT
        ),
        name="reduce_dkv",
    )(dk, dv)


def local(queries, keys, values, outputs, out_grad, lse, block_order, doc_lengths):
    me = lax.axis_index("ctx").astype(I32)
    plane = (me // 4) % 2
    swap = [(i, i ^ 4) for i in range(32)]
    pair_q = lax.ppermute(queries, "ctx", swap)
    pair_g = lax.ppermute(out_grad, "ctx", swap)
    ka, va, delta, pair_delta, pair_lse = gather(keys, values, out_grad, outputs, lse)
    k = ka.reshape(2 * PLANE, B, D)
    v = va.reshape(2 * PLANE, B, D)
    own = jnp.stack([me, plane])
    other = jnp.stack([me ^ 4, plane])
    dq_own, dk, dv = attend(own, block_order, doc_lengths, queries, out_grad, lse, delta, k, v)
    dq_pair, dk, dv = attend(
        other, block_order, doc_lengths, pair_q, pair_g, pair_lse, pair_delta, k, v, (dk, dv)
    )
    dq_back = lax.ppermute(dq_pair, "ctx", swap)
    key_grad, value_grad = reduce(dk.reshape(PLANE, T, D), dv.reshape(PLANE, T, D))
    query_grad = (jnp.float32(D**-0.5) * (dq_own + dq_back.astype(F32))).astype(BF)
    return (query_grad, key_grad, value_grad)


def solution(mesh):
    rows = P(("dp", "ctx"), None)
    return jax.shard_map(
        local,
        mesh=mesh,
        in_specs=(rows, rows, rows, rows, rows, P(None, ("dp", "ctx")), P("dp"), P("dp")),
        out_specs=(rows, rows, rows),
        check_vma=False,
    )
```

```python
import jax
import jax.numpy as jnp
from jax import lax
from jax.experimental import pallas as pl
from jax.experimental.pallas import tpu as pltpu
from jax.sharding import PartitionSpec as P

BF = jnp.bfloat16
F32 = jnp.float32
I32 = jnp.int32
MESH = pl.DeviceIdType.MESH
VM = pl.BlockSpec(memory_space=pltpu.VMEM)
SM = pl.BlockSpec(memory_space=pltpu.SMEM)
ANY = pl.BlockSpec(memory_space=pl.ANY)

RING = 4
PLANE = RING * RING
T = 256
B = 128
H = 8
D = 128
VMEM_LIMIT = 32 * 2**20


def dot(a, b, ca, cb):
    return lax.dot_general(a, b, (((ca,), (cb,)), ((), ())), preferred_element_type=F32)


def stay(array):
    return pltpu.with_memory_space_constraint(array, pltpu.HBM)


def coords():
    me = lax.axis_index("ctx")
    return me // 8, (me // 4) % 2, me % 4


def ident(z, y, x):
    return {"ctx": z * 8 + y * 4 + x}


def step_of(v, d):
    return lax.rem(v + d, RING)


def greet(z, y, x, pair):
    barrier = pltpu.get_barrier_semaphore()
    others = [ident(z, y, step_of(x, d)) for d in (1, 2, 3)]
    others += [ident(step_of(z, d), y, x) for d in (1, 2, 3)]
    if pair:
        others.append(ident(z, 1 - y, x))
    for other in others:
        pl.semaphore_signal(barrier, inc=1, device_id=other, device_id_type=MESH)
    pl.semaphore_wait(barrier, len(others))


def gather_kernel(
    k_ref, v_ref, q_ref, g_ref, o_ref, lse_ref, ka, va, qa, ga, qt, gt, lses, deltas,
    outs, own_sem, s1, r1, s2, r2, ps, pr,
):
    z, y, x = coords()
    here = z * RING + x
    pair = ident(z, 1 - y, x)

    def keep(src, dst, sem):
        copy = pltpu.make_async_copy(src, dst, sem)
        copy.start()
        return copy

    grads_in = [keep(g_ref.at[pl.ds(blk * B, B)], ga.at[blk], own_sem.at[blk]) for blk in (0, 1)]
    outs_in = keep(o_ref, outs, own_sem.at[2])
    lse_in = keep(lse_ref, lses.at[0], own_sem.at[3])
    rows_in = [keep(q_ref.at[pl.ds(blk * B, B)], qa.at[blk], own_sem.at[4 + blk]) for blk in (0, 1)]
    own = [keep(src, dst.at[here], own_sem.at[6 + a]) for a, (src, dst) in enumerate(((k_ref, ka), (v_ref, va)))]
    greet(z, y, x, True)

    def send(src, dst, ssem, rsem, to):
        copy = pltpu.make_async_remote_copy(
            src_ref=src, dst_ref=dst, send_sem=ssem, recv_sem=rsem, device_id=to, device_id_type=MESH
        )
        copy.start()
        return copy

    srcs, alls = (k_ref, v_ref), (ka, va)

    def first_peer(a, d):
        return ident(z, y, step_of(x, d)) if a == 0 else ident(step_of(z, d), y, x)

    def second_peer(a, d):
        return first_peer(1 - a, d)

    def slot_from(a, s):
        return z * RING + step_of(x, RING - s) if a == 0 else step_of(z, RING - s) * RING + x

    first, second = {}, {}
    for a in (0, 1):
        for d in (1, 3, 2):
            first[a, d] = send(srcs[a], alls[a].at[here], s1.at[a, d - 1], r1.at[a, d - 1], first_peer(a, d))
    across = [send(lse_ref, lses.at[1], ps.at[4], pr.at[4], pair)]
    for blk in (0, 1):
        for i, (src, dst) in enumerate(((q_ref, qa), (g_ref, ga))):
            n = 2 * blk + i
            across.append(send(src.at[pl.ds(blk * B, B)], dst.at[2 + blk], ps.at[n], pr.at[n], pair))
    for a in (0, 1):
        for d in (1, 3, 2):
            second[a, 0, d] = send(srcs[a], alls[a].at[here], s2.at[a, 0, d - 1], r2.at[a, 0, d - 1], second_peer(a, d))
    for copy in grads_in + [outs_in]:
        copy.wait()
    ones = jnp.ones((8, D), BF)
    for h in range(H):
        cols = slice(h * D, (h + 1) * D)
        grad = jnp.concatenate([ga[0, :, cols], ga[1, :, cols]], axis=0)
        prod = grad.astype(F32) * outs[:, cols].astype(F32)
        hi = prod.astype(BF)
        lo = (prod - hi.astype(F32)).astype(BF)
        total = dot(ones, hi, 1, 1) + dot(ones, lo, 1, 1)
        deltas[0, h : h + 1, :] = total[0:1, :]
    across.append(send(deltas.at[0], deltas.at[1], ps.at[5], pr.at[5], pair))

    for s in (1, 3, 2):
        for a in (0, 1):
            first[a, s].wait_recv()
            block = alls[a].at[slot_from(a, s)]
            for d in (1, 3, 2):
                second[a, s, d] = send(block, block, s2.at[a, s, d - 1], r2.at[a, s, d - 1], second_peer(a, d))

    def turn(src, dst, blk):
        for h in range(H):
            cols = slice(h * D, (h + 1) * D)
            dst[blk, :, cols] = src[blk, :, cols].T

    for copy in own + rows_in + [lse_in]:
        copy.wait()
    for blk in (0, 1):
        turn(qa, qt, blk)
        turn(ga, gt, blk)
    for copy in second.values():
        copy.wait_recv()
    across[0].wait_recv()
    across[5].wait_recv()
    for blk in (0, 1):
        across[1 + 2 * blk].wait_recv()
        turn(qa, qt, 2 + blk)
        across[2 + 2 * blk].wait_recv()
        turn(ga, gt, 2 + blk)
    for copy in list(first.values()) + list(second.values()) + across:
        copy.wait_send()


def gather(keys, values, queries, out_grad, outputs, lse):
    dma = pltpu.SemaphoreType.DMA
    return pl.pallas_call(
        gather_kernel,
        out_shape=(
            pltpu.VMEM((PLANE, T, D), BF),
            pltpu.VMEM((PLANE, T, D), BF),
            pltpu.VMEM((4, B, H * D), BF),
            pltpu.VMEM((4, B, H * D), BF),
            pltpu.VMEM((4, D, H * B), BF),
            pltpu.VMEM((4, D, H * B), BF),
            pltpu.VMEM((2, H, T), F32),
            pltpu.VMEM((2, H, T), F32),
        ),
        in_specs=[ANY] * 6,
        out_specs=(VM,) * 8,
        scratch_shapes=[
            pltpu.VMEM((T, H * D), BF),
            dma((8,)), dma((2, 3)), dma((2, 3)), dma((2, 4, 3)), dma((2, 4, 3)), dma((6,)), dma((6,)),
        ],
        compiler_params=pltpu.CompilerParams(
            collective_id=0, has_side_effects=True, vmem_limit_bytes=VMEM_LIMIT
        ),
        name="gather_rows",
    )(*[stay(t) for t in (keys, values, queries, out_grad, outputs, lse)])


def attend_kernel(
    order, lens, qa, ga, qt, gt, lse_ref, delta_ref, k_ref, v_ref, dq_own, dq_pair, dk_out, dv_out,
    inv, ends, item_q, item_a, item_b, pos_a, pos_b, lc, dc, qfrom, qbase, dqa, dk, dv, pbuf, dbuf,
):
    me = lax.axis_index("ctx")
    plane = (me // 4) % 2
    mate = me + 4 - 8 * plane
    dk[...] = jnp.zeros_like(dk)
    dv[...] = jnp.zeros_like(dv)

    def invert(s, c):
        inv[order[s]] = s
        return c

    lax.fori_loop(0, 64, invert, 0)

    def add_end(d, c):
        c = c + lens[d]
        ends[d] = c
        return c

    lax.fori_loop(0, 16, add_end, jnp.int32(0))
    row = lax.broadcasted_iota(I32, (B, D), 0)

    count = jnp.int32(0)
    for blk in range(4):
        at = order[(me, mate)[blk // 2] * 2 + blk % 2]
        base = at * B
        places = base + row
        begin = jnp.zeros_like(places)
        low = jnp.int32(0)
        for d in range(16):
            begin = jnp.where(ends[d] <= places, ends[d], begin)
            low = jnp.where(ends[d] <= base, ends[d], low)
        qfrom[blk] = begin
        qbase[blk] = base

        def visit(p, c):
            n, half = c
            s = inv[p]
            dev = s // 2
            mine = (dev // 4) % 2 == plane
            slot = ((dev // 8) * RING + dev % 4) * 2 + s % 2

            @pl.when(mine & (half == 0))
            def _():
                item_q[n] = blk
                item_a[n] = slot
                pos_a[n] = p * B
                item_b[n] = 0
                pos_b[n] = 1 << 20

            @pl.when(mine & (half == 1))
            def _():
                item_b[n] = slot
                pos_b[n] = p * B

            full = mine & (half == 1)
            return jnp.where(full, n + 1, n), jnp.where(mine, 1 - half, half)

        n, half = lax.fori_loop(low // B, at + 1, visit, (count, jnp.int32(0)))
        count = n + half

    item_q[count] = 0
    item_a[count] = 0
    item_b[count] = 0
    pos_a[count] = 1 << 20
    pos_b[count] = 1 << 20

    head_of = lax.broadcasted_iota(I32, (3 * H, D), 0) % H

    def pieces(ref, side, rows):
        whole = jnp.minimum(ref[side, :, rows], 1e30)
        hi = whole.astype(BF)
        left = whole - hi.astype(F32)
        mid = left.astype(BF)
        lo = (left - mid.astype(F32)).astype(BF)
        return jnp.concatenate([hi.astype(F32), mid.astype(F32), lo.astype(F32)], axis=0).astype(BF)

    for blk in range(4):
        rows = slice(blk % 2 * B, (blk % 2 + 1) * B)
        lse_parts = pieces(lse_ref, blk // 2, rows)
        delta_parts = pieces(delta_ref, blk // 2, rows)
        for h in range(H):
            cols = slice(h * D, (h + 1) * D)
            select = jnp.where(head_of == h, 1.0, 0.0).astype(BF)
            lc[blk, cols, :] = dot(lse_parts, select, 0, 0)
            dc[blk, cols, :] = dot(delta_parts, select, 0, 0)
    dqa[...] = jnp.zeros_like(dqa)
    scale = jnp.float32(D**-0.5)
    across = lax.broadcasted_iota(I32, (1, B), 1)

    def load(n):
        a, b = item_a[n], item_b[n]
        return (
            jnp.concatenate([k_ref[a], k_ref[b]], axis=0),
            jnp.concatenate([v_ref[a], v_ref[b]], axis=0),
        )

    def scores(n, par, kk, vv):
        blk = item_q[n]
        key_pos = jnp.concatenate([pos_a[n] + across, pos_b[n] + across], axis=1)
        here = qbase[blk] + row
        here = jnp.concatenate([here, here], axis=1)
        begin = qfrom[blk]
        begin = jnp.concatenate([begin, begin], axis=1)
        allowed = (key_pos <= here) & (key_pos >= begin)
        allowed = jnp.concatenate([allowed, allowed], axis=0)
        for two in range(4):
            cols = slice(two * 256, (two + 1) * 256)
            heads = [slice((2 * two + i) * D, (2 * two + i + 1) * D) for i in (0, 1)]
            score = dot(jnp.concatenate([qa[blk, :, c] for c in heads], axis=0), kk, 1, 1)
            dprob = dot(jnp.concatenate([ga[blk, :, c] for c in heads], axis=0), vv, 1, 1)
            less = lc[blk, cols, :]
            delta = dc[blk, cols, :]
            prob = jnp.where(allowed, jnp.exp(score * scale - jnp.concatenate([less, less], axis=1)), 0.0)
            pbuf[par, cols, :] = prob.astype(BF)
            dbuf[par, cols, :] = (prob * (dprob - jnp.concatenate([delta, delta], axis=1))).astype(BF)

    def grads(n, par, kk):
        blk, a, b = item_q[n], item_a[n], item_b[n]
        dqa[blk] += jnp.dot(dbuf[par], kk, preferred_element_type=F32)
        dv_term = jnp.dot(gt[blk], pbuf[par], preferred_element_type=F32)
        dk_term = jnp.dot(qt[blk], dbuf[par], preferred_element_type=F32)
        dk[a] += dk_term[:, :B]
        dk[b] += dk_term[:, B:]
        dv[a] += dv_term[:, :B]
        dv[b] += dv_term[:, B:]

    def two(i, c):
        k0, v0 = load(2 * i)
        k1, v1 = load(2 * i + 1)
        scores(2 * i, 0, k0, v0)
        scores(2 * i + 1, 1, k1, v1)
        grads(2 * i, 0, k0)
        grads(2 * i + 1, 1, k1)
        return c

    lax.fori_loop(0, (count + 1) // 2, two, 0)

    for blk in range(4):
        dst = (dq_own, dq_pair)[blk // 2]
        for h in range(H):
            cols = slice(h * D, (h + 1) * D)
            dst[blk % 2, :, cols] = dqa[blk, cols, :].astype(dst.dtype)
    dk_out[...] = dk[...].astype(BF)
    dv_out[...] = dv[...].astype(BF)


def attend(order, lens, *arrays):
    return pl.pallas_call(
        attend_kernel,
        out_shape=(
            pltpu.VMEM((2, B, H * D), F32),
            pltpu.VMEM((2, B, H * D), BF),
            pltpu.VMEM((2 * PLANE, D, B), BF),
            pltpu.VMEM((2 * PLANE, D, B), BF),
        ),
        in_specs=[SM] * 2 + [VM] * 8,
        out_specs=(VM,) * 4,
        scratch_shapes=[
            pltpu.SMEM((64,), I32),
            pltpu.SMEM((16,), I32),
            pltpu.SMEM((80,), I32),
            pltpu.SMEM((80,), I32),
            pltpu.SMEM((80,), I32),
            pltpu.SMEM((80,), I32),
            pltpu.SMEM((80,), I32),
            pltpu.VMEM((4, H * B, D), F32),
            pltpu.VMEM((4, H * B, D), F32),
            pltpu.VMEM((4, B, D), I32),
            pltpu.SMEM((4,), I32),
            pltpu.VMEM((4, H * B, D), F32),
            pltpu.VMEM((2 * PLANE, D, B), F32),
            pltpu.VMEM((2 * PLANE, D, B), F32),
            pltpu.VMEM((2, H * B, 2 * B), BF),
            pltpu.VMEM((2, H * B, 2 * B), BF),
        ],
        compiler_params=pltpu.CompilerParams(vmem_limit_bytes=VMEM_LIMIT),
        name="attend",
    )(stay(order), stay(lens), *arrays)


def reduce_kernel(dq_ref, dk_ref, dv_ref, back, k_sum, v_sum, in1, out2, in2, s1, r1, s2, r2, ps, pr):
    z, y, x = coords()
    greet(z, y, x, True)
    srcs = (dk_ref, dv_ref)

    def send(src, dst, ssem, rsem, to):
        copy = pltpu.make_async_remote_copy(
            src_ref=src, dst_ref=dst, send_sem=ssem, recv_sem=rsem, device_id=to, device_id_type=MESH
        )
        copy.start()
        return copy

    def first_peer(a, d):
        return ident(step_of(z, d), y, x) if a == 0 else ident(z, y, step_of(x, d))

    def second_peer(a, e):
        return first_peer(1 - a, e)

    def slot(a, d, e):
        if a == 0:
            return step_of(z, d) * RING + step_of(x, e)
        return step_of(z, e) * RING + step_of(x, d)

    first, second = {}, {}
    for e in (2, 1, 3, 0):
        for a in (0, 1):
            for d in (2, 1, 3):
                first[a, e, d] = send(
                    srcs[a].at[slot(a, d, e)], in1.at[a, e, d - 1], s1.at[a, e, d - 1], r1.at[a, e, d - 1],
                    first_peer(a, d),
                )
    across = send(dq_ref, back, ps, pr, ident(z, 1 - y, x))
    sums = []
    for e in (2, 1, 3, 0):
        for a in (0, 1):
            total = srcs[a][slot(a, 0, e)].astype(F32)
            for d in (1, 2, 3):
                first[a, e, d].wait_recv()
                total = total + in1[a, e, d - 1].astype(F32)
            if e:
                out2[a, e - 1] = total.astype(BF)
                second[a, e] = send(out2.at[a, e - 1], in2.at[a, e - 1], s2.at[a, e - 1], r2.at[a, e - 1], second_peer(a, e))
            else:
                sums.append(total)
    for a, dst in ((0, k_sum), (1, v_sum)):
        total = sums[a]
        for e in (1, 2, 3):
            second[a, e].wait_recv()
            total = total + in2[a, e - 1].astype(F32)
        dst[...] = total
    across.wait()
    for copy in list(first.values()) + list(second.values()):
        copy.wait_send()


def reduce(dq, dk, dv):
    dma = pltpu.SemaphoreType.DMA
    return pl.pallas_call(
        reduce_kernel,
        out_shape=(
            pltpu.VMEM((2, B, H * D), BF),
            pltpu.VMEM((2, D, B), F32),
            pltpu.VMEM((2, D, B), F32),
        ),
        in_specs=[VM] * 3,
        out_specs=(VM,) * 3,
        scratch_shapes=[
            pltpu.VMEM((2, 4, 3, 2, D, B), BF),
            pltpu.VMEM((2, 3, 2, D, B), BF),
            pltpu.VMEM((2, 3, 2, D, B), BF),
            dma((2, 4, 3)), dma((2, 4, 3)), dma((2, 3)), dma((2, 3)), dma, dma,
        ],
        compiler_params=pltpu.CompilerParams(
            collective_id=1, has_side_effects=True, vmem_limit_bytes=VMEM_LIMIT
        ),
        name="reduce_rows",
    )(dq, dk.reshape(PLANE, 2, D, B), dv.reshape(PLANE, 2, D, B))


def finish_kernel(dq_own, back, k_sum, v_sum, query_ref, key_ref, value_ref):
    scale = jnp.float32(D**-0.5)
    for blk in (0, 1):
        rows = slice(blk * B, (blk + 1) * B)
        query_ref[rows, :] = (scale * (dq_own[blk] + back[blk].astype(F32))).astype(BF)
        key_ref[rows, :] = (scale * k_sum[blk]).T.astype(BF)
        value_ref[rows, :] = v_sum[blk].T.astype(BF)


def finish(*arrays):
    grad = jax.ShapeDtypeStruct((T, D), BF)
    return pl.pallas_call(
        finish_kernel,
        out_shape=(jax.ShapeDtypeStruct((T, H * D), BF), grad, grad),
        in_specs=[VM] * 4,
        out_specs=(VM,) * 3,
        compiler_params=pltpu.CompilerParams(vmem_limit_bytes=VMEM_LIMIT),
        name="finish",
    )(*arrays)


def local(queries, keys, values, outputs, out_grad, lse, block_order, doc_lengths):
    ka, va, qa, ga, qt, gt, lses, deltas = gather(keys, values, queries, out_grad, outputs, lse)
    k = ka.reshape(2 * PLANE, B, D)
    v = va.reshape(2 * PLANE, B, D)
    dq_own, dq_pair, dk, dv = attend(block_order, doc_lengths, qa, ga, qt, gt, lses, deltas, k, v)
    back, k_sum, v_sum = reduce(dq_pair, dk, dv)
    return finish(dq_own, back, k_sum, v_sum)


def solution(mesh):
    rows = P(("dp", "ctx"), None)
    return jax.shard_map(
        local,
        mesh=mesh,
        in_specs=(rows, rows, rows, rows, rows, P(None, ("dp", "ctx")), P("dp"), P("dp")),
        out_specs=(rows, rows, rows),
        check_vma=False,
    )
```

```python
import functools

import jax
import jax.numpy as jnp
from jax import lax
from jax.experimental import pallas as pl
from jax.experimental.pallas import tpu as pltpu
from jax.sharding import PartitionSpec as P

BF = jnp.bfloat16
F32 = jnp.float32
I32 = jnp.int32
MESH = pl.DeviceIdType.MESH
VM = pl.BlockSpec(memory_space=pltpu.VMEM)
SM = pl.BlockSpec(memory_space=pltpu.SMEM)
ANY = pl.BlockSpec(memory_space=pl.ANY)

RING = 4
PLANE = RING * RING
T = 256
B = 128
H = 8
D = 128
VMEM_LIMIT = 32 * 2**20


def dot(a, b, ca, cb):
    return lax.dot_general(a, b, (((ca,), (cb,)), ((), ())), preferred_element_type=F32)


def stay(array):
    return pltpu.with_memory_space_constraint(array, pltpu.HBM)


def coords():
    me = lax.axis_index("ctx")
    return me // 8, (me // 4) % 2, me % 4


def ident(z, y, x):
    return {"ctx": z * 8 + y * 4 + x}


def step_of(v, d):
    return lax.rem(v + d, RING)


def greet_signal(z, y, x):
    barrier = pltpu.get_barrier_semaphore()
    others = [ident(z, y, step_of(x, d)) for d in (1, 2, 3)]
    others += [ident(step_of(z, d), y, x) for d in (1, 2, 3)]
    others.append(ident(z, 1 - y, x))
    for other in others:
        pl.semaphore_signal(barrier, inc=1, device_id=other, device_id_type=MESH)


def greet_wait():
    pl.semaphore_wait(pltpu.get_barrier_semaphore(), 7)


def widen(ref, dst):
    head_of = lax.broadcasted_iota(I32, (3 * H, D), 0) % H
    for blk in (0, 1):
        whole = jnp.minimum(ref[:, blk * B : (blk + 1) * B], 1e30)
        hi = whole.astype(BF)
        left = whole - hi.astype(F32)
        mid = left.astype(BF)
        lo = (left - mid.astype(F32)).astype(BF)
        parts = jnp.concatenate([hi.astype(F32), mid.astype(F32), lo.astype(F32)], axis=0).astype(BF)
        for h in range(H):
            select = jnp.where(head_of == h, 1.0, 0.0).astype(BF)
            dst[blk, h * D : (h + 1) * D, :] = dot(parts, select, 0, 0)


def gather_kernel(
    k_ref, v_ref, q_ref, g_ref, o_ref, lse_ref, ka, va, qa, ga, qt, gt, lc, dc, delta,
    outs, lses, own_sem, s1, r1, s2, r2, s3, r3,
):
    z, y, x = coords()
    here = z * RING + x

    def keep(src, dst, sem):
        copy = pltpu.make_async_copy(src, dst, sem)
        copy.start()
        return copy

    grads_in = [keep(g_ref.at[pl.ds(blk * B, B)], ga.at[blk], own_sem.at[blk]) for blk in (0, 1)]
    outs_in = keep(o_ref, outs, own_sem.at[2])
    lse_in = keep(lse_ref, lses, own_sem.at[3])
    rows_in = [keep(q_ref.at[pl.ds(blk * B, B)], qa.at[blk], own_sem.at[4 + blk]) for blk in (0, 1)]
    own = [keep(src, dst.at[here], own_sem.at[6 + a]) for a, (src, dst) in enumerate(((k_ref, ka), (v_ref, va)))]
    greet_signal(z, y, x)
    greet_wait()

    def send(src, dst, ssem, rsem, to):
        copy = pltpu.make_async_remote_copy(
            src_ref=src, dst_ref=dst, send_sem=ssem, recv_sem=rsem, device_id=to, device_id_type=MESH
        )
        copy.start()
        return copy

    srcs, alls = (k_ref, v_ref), (ka, va)

    def first_peer(a, d):
        return ident(z, y, step_of(x, d)) if a == 0 else ident(step_of(z, d), y, x)

    def second_peer(a, d):
        return first_peer(1 - a, d)

    def slot_from(a, s, t=0):
        if a == 0:
            return step_of(z, RING - t) * RING + step_of(x, RING - s)
        return step_of(z, RING - s) * RING + step_of(x, RING - t)

    first, second, third = {}, {}, {}

    def spread(a, s):
        src = srcs[a] if s == 0 else alls[a].at[slot_from(a, s)]
        dst = alls[a].at[here if s == 0 else slot_from(a, s)]
        for e in (1, 3):
            second[a, s, e] = send(src, dst, s2.at[a, s, e - 1], r2.at[a, s, e - 1], second_peer(a, e))

    for d in (1, 3, 2):
        for a in (0, 1):
            first[a, d] = send(srcs[a], alls[a].at[here], s1.at[a, d - 1], r1.at[a, d - 1], first_peer(a, d))
    for a in (0, 1):
        spread(a, 0)

    for s in (1, 3, 2):
        for a in (0, 1):
            first[a, s].wait_recv()
            spread(a, s)

    for copy in grads_in + [outs_in]:
        copy.wait()
    ones = jnp.ones((8, D), BF)
    for h in range(H):
        cols = slice(h * D, (h + 1) * D)
        grad = jnp.concatenate([ga[0, :, cols], ga[1, :, cols]], axis=0)
        prod = grad.astype(F32) * outs[:, cols].astype(F32)
        hi = prod.astype(BF)
        lo = (prod - hi.astype(F32)).astype(BF)
        total = dot(ones, hi, 1, 1) + dot(ones, lo, 1, 1)
        delta[h : h + 1, :] = total[0:1, :]

    def relay(s):
        for e, half in ((1, 0), (3, 1)):
            for a in (0, 1):
                second[a, s, e].wait_recv()
                part = alls[a].at[slot_from(a, s, e), pl.ds(half * B, B)]
                third[a, s, half] = send(part, part, s3.at[a, s, half], r3.at[a, s, half], second_peer(a, e))

    def turn(src, dst, blk):
        for h in range(H):
            cols = slice(h * D, (h + 1) * D)
            dst[blk, :, cols] = src[blk, :, cols].T

    relay(0)
    for copy in rows_in + own:
        copy.wait()
    turn(qa, qt, 0)
    turn(ga, gt, 0)
    relay(1)
    turn(qa, qt, 1)
    turn(ga, gt, 1)
    relay(3)
    lse_in.wait()
    widen(lses, lc)
    widen(delta, dc)
    relay(2)
    for copy in third.values():
        copy.wait_recv()
    for copy in list(first.values()) + list(second.values()) + list(third.values()):
        copy.wait_send()


def gather(keys, values, queries, out_grad, outputs, lse):
    dma = pltpu.SemaphoreType.DMA
    return pl.pallas_call(
        gather_kernel,
        out_shape=(
            pltpu.VMEM((PLANE, T, D), BF),
            pltpu.VMEM((PLANE, T, D), BF),
            pltpu.VMEM((2, B, H * D), BF),
            pltpu.VMEM((2, B, H * D), BF),
            pltpu.VMEM((2, D, H * B), BF),
            pltpu.VMEM((2, D, H * B), BF),
            pltpu.VMEM((2, H * B, D), F32),
            pltpu.VMEM((2, H * B, D), F32),
            pltpu.VMEM((H, T), F32),
        ),
        in_specs=[ANY] * 6,
        out_specs=(VM,) * 9,
        scratch_shapes=[
            pltpu.VMEM((T, H * D), BF),
            pltpu.VMEM((H, T), F32),
            dma((8,)), dma((2, 3)), dma((2, 3)), dma((2, 4, 3)), dma((2, 4, 3)),
            dma((2, 4, 2)), dma((2, 4, 2)),
        ],
        compiler_params=pltpu.CompilerParams(
            collective_id=0, has_side_effects=True, vmem_limit_bytes=VMEM_LIMIT
        ),
        name="gather_rows",
    )(*[stay(t) for t in (keys, values, queries, out_grad, outputs, lse)])


KEYS = 36
NEVER = 1 << 20


def attend_kernel(own, order, lens, *refs):
    if own:
        qa, ga, qt, gt, lc, dc, k_ref, v_ref, dqa, dk, dv = refs[:11]
        slots, places, qfrom, qbase, pbuf, dbuf = refs[11:]
    else:
        q_hbm, g_hbm, lse_ref, delta_ref, k_ref, v_ref, _, _, dq_out, dk, dv = refs[:11]
        slots, places, qfrom, qbase, pbuf, dbuf, qa, ga, qt, gt, lc, dc, dqa, sems = refs[11:]
        loads = []
        for blk in (0, 1):
            for i, (src, dst) in enumerate(((q_hbm, qa), (g_hbm, ga))):
                copy = pltpu.make_async_copy(src.at[pl.ds(blk * B, B)], dst.at[blk], sems.at[2 * blk + i])
                copy.start()
                loads.append(copy)
    me = lax.axis_index("ctx")
    plane = (me // 4) % 2
    owner = me if own else me + 4 - 8 * plane

    ats = [order[owner * 2 + blk] for blk in (0, 1)]
    row = lax.broadcasted_iota(I32, (B, D), 0)
    lows = [jnp.int32(0), jnp.int32(0)]
    begins = [jnp.zeros_like(row), jnp.zeros_like(row)]
    end = jnp.int32(0)
    for d in range(lens.shape[0]):
        end = end + lens[d]
        for blk in (0, 1):
            lows[blk] = jnp.where(end <= ats[blk] * B, end, lows[blk])
            begins[blk] = jnp.where(end <= ats[blk] * B + row, end, begins[blk])
    lows = [low // B for low in lows]
    for blk in (0, 1):
        qfrom[blk] = begins[blk]
        qbase[blk] = ats[blk] * B

    def list_keys(i, counts):
        counts = list(counts)
        for j in range(8):
            slot = i * 8 + j
            p = order[i * 16 + plane * 8 + j]
            for blk in (0, 1):
                slots[blk * KEYS + counts[blk]] = slot
                places[blk * KEYS + counts[blk]] = p * B
                needed = (p >= lows[blk]) & (p <= ats[blk])
                counts[blk] = counts[blk] + needed.astype(I32)
        return tuple(counts)

    counts = lax.fori_loop(0, 4, list_keys, (jnp.int32(0), jnp.int32(0)))
    for blk in (0, 1):
        for i in range(3):
            slots[blk * KEYS + counts[blk] + i] = 0
            places[blk * KEYS + counts[blk] + i] = NEVER
    items = [(count + 1) // 2 for count in counts]
    total = items[0] + items[1]

    dqa[...] = jnp.zeros_like(dqa)
    if own:
        dk[...] = jnp.zeros_like(dk)
        dv[...] = jnp.zeros_like(dv)
    else:
        widen(lse_ref, lc)
        widen(delta_ref, dc)
        for blk in (0, 1):
            for src, dst, copy in ((qa, qt, loads[2 * blk]), (ga, gt, loads[2 * blk + 1])):
                copy.wait()
                for h in range(H):
                    cols = slice(h * D, (h + 1) * D)
                    dst[blk, :, cols] = src[blk, :, cols].T
    scale = jnp.float32(D**-0.5)
    across = lax.broadcasted_iota(I32, (1, B), 1)

    def load(n):
        later = (n >= items[0]).astype(I32)
        at = later * (KEYS - 2 * items[0]) + 2 * n
        a, b = slots[at], slots[at + 1]
        kk = jnp.concatenate([k_ref[a], k_ref[b]], axis=0)
        vv = jnp.concatenate([v_ref[a], v_ref[b]], axis=0)
        return later, a, b, kk, vv, places[at], places[at + 1]

    def scores(item, par):
        blk, _, _, kk, vv, place_a, place_b = item
        key_pos = jnp.concatenate([place_a + across, place_b + across], axis=1)
        here = qbase[blk] + row
        here = jnp.concatenate([here, here], axis=1)
        begin = qfrom[blk]
        begin = jnp.concatenate([begin, begin], axis=1)
        allowed = (key_pos <= here) & (key_pos >= begin)
        allowed = jnp.concatenate([allowed, allowed], axis=0)
        for two in range(4):
            cols = slice(two * 256, (two + 1) * 256)
            heads = [slice((2 * two + i) * D, (2 * two + i + 1) * D) for i in (0, 1)]
            score = dot(jnp.concatenate([qa[blk, :, c] for c in heads], axis=0), kk, 1, 1)
            dprob = dot(jnp.concatenate([ga[blk, :, c] for c in heads], axis=0), vv, 1, 1)
            less = lc[blk, cols, :]
            delta = dc[blk, cols, :]
            prob = jnp.where(allowed, jnp.exp(score * scale - jnp.concatenate([less, less], axis=1)), 0.0)
            pbuf[par, cols, :] = prob.astype(BF)
            dbuf[par, cols, :] = (prob * (dprob - jnp.concatenate([delta, delta], axis=1))).astype(BF)

    def grads(item, par):
        blk, a, b, kk = item[:4]
        dqa[blk] += jnp.dot(dbuf[par], kk, preferred_element_type=F32)
        dv_term = jnp.dot(gt[blk], pbuf[par], preferred_element_type=F32)
        dk_term = jnp.dot(qt[blk], dbuf[par], preferred_element_type=F32)
        dk[a] += dk_term[:, :B]
        dk[b] += dk_term[:, B:]
        dv[a] += dv_term[:, :B]
        dv[b] += dv_term[:, B:]

    def two(i, c):
        now = [load(2 * i), load(2 * i + 1)]
        for par in (0, 1):
            scores(now[par], par)
        for par in (0, 1):
            grads(now[par], par)
        return c

    lax.fori_loop(0, (total + 1) // 2, two, 0)
    if not own:
        dq_out[...] = dqa[...].astype(BF)


def attend(own, order, lens, *arrays):
    sums = pltpu.VMEM((2 * PLANE, D, B), F32)
    rows = pltpu.VMEM((2, B, H * D), BF)
    cols = pltpu.VMEM((2, D, H * B), BF)
    scratch = [
        pltpu.SMEM((2 * KEYS,), I32),
        pltpu.SMEM((2 * KEYS,), I32),
        pltpu.VMEM((2, B, D), I32),
        pltpu.SMEM((2,), I32),
        pltpu.VMEM((2, H * B, 2 * B), BF),
        pltpu.VMEM((2, H * B, 2 * B), BF),
    ]
    if own:
        specs = [SM] * 2 + [VM] * 8
    else:
        specs = [SM] * 2 + [ANY] * 2 + [VM] * 6
        scratch += [rows, rows, cols, cols] + [pltpu.VMEM((2, H * B, D), F32)] * 3 + [pltpu.SemaphoreType.DMA((4,))]
        arrays = [stay(t) for t in arrays[:2]] + list(arrays[2:])
    return pl.pallas_call(
        functools.partial(attend_kernel, own),
        out_shape=(pltpu.VMEM((2, H * B, D), F32 if own else BF), sums, sums),
        in_specs=specs,
        out_specs=(VM,) * 3,
        scratch_shapes=scratch,
        input_output_aliases={} if own else {8: 1, 9: 2},
        compiler_params=pltpu.CompilerParams(vmem_limit_bytes=VMEM_LIMIT),
        name="attend_own" if own else "attend_pair",
    )(stay(order), stay(lens), *arrays)


def reduce_kernel(dq_ref, dk_ref, dv_ref, back, k_sum, v_sum, out1, in1, out2, in2, s1, r1, s2, r2, ps, pr):
    z, y, x = coords()
    greet_signal(z, y, x)
    srcs = (dk_ref, dv_ref)
    for a in (0, 1):
        out1[a] = srcs[a][...].astype(BF)
    greet_wait()

    def send(src, dst, ssem, rsem, to):
        copy = pltpu.make_async_remote_copy(
            src_ref=src, dst_ref=dst, send_sem=ssem, recv_sem=rsem, device_id=to, device_id_type=MESH
        )
        copy.start()
        return copy

    def first_peer(a, d):
        return ident(step_of(z, d), y, x) if a == 0 else ident(z, y, step_of(x, d))

    def second_peer(a, e):
        return first_peer(1 - a, e)

    def slot(a, d, e):
        if a == 0:
            return step_of(z, d) * RING + step_of(x, e)
        return step_of(z, e) * RING + step_of(x, d)

    first, second = {}, {}
    for e in (2, 1, 3, 0):
        for a in (0, 1):
            for d in (2, 1, 3):
                first[a, e, d] = send(
                    out1.at[a, slot(a, d, e)], in1.at[a, e, d - 1], s1.at[a, e, d - 1], r1.at[a, e, d - 1],
                    first_peer(a, d),
                )
    across = send(dq_ref, back, ps, pr, ident(z, 1 - y, x))
    sums = []
    for e in (2, 1, 3, 0):
        for a in (0, 1):
            total = srcs[a][slot(a, 0, e)]
            for d in (1, 2, 3):
                first[a, e, d].wait_recv()
                total = total + in1[a, e, d - 1].astype(F32)
            if e:
                out2[a, e - 1] = total.astype(BF)
                second[a, e] = send(out2.at[a, e - 1], in2.at[a, e - 1], s2.at[a, e - 1], r2.at[a, e - 1], second_peer(a, e))
            else:
                sums.append(total)
    for a, dst in ((0, k_sum), (1, v_sum)):
        total = sums[a]
        for e in (1, 2, 3):
            second[a, e].wait_recv()
            total = total + in2[a, e - 1].astype(F32)
        dst[...] = total
    across.wait()
    for copy in list(first.values()) + list(second.values()):
        copy.wait_send()


def reduce(dq, dk, dv):
    dma = pltpu.SemaphoreType.DMA
    return pl.pallas_call(
        reduce_kernel,
        out_shape=(
            pltpu.VMEM((2, H * B, D), BF),
            pltpu.VMEM((2, D, B), F32),
            pltpu.VMEM((2, D, B), F32),
        ),
        in_specs=[VM] * 3,
        out_specs=(VM,) * 3,
        scratch_shapes=[
            pltpu.VMEM((2, PLANE, 2, D, B), BF),
            pltpu.VMEM((2, 4, 3, 2, D, B), BF),
            pltpu.VMEM((2, 3, 2, D, B), BF),
            pltpu.VMEM((2, 3, 2, D, B), BF),
            dma((2, 4, 3)), dma((2, 4, 3)), dma((2, 3)), dma((2, 3)), dma, dma,
        ],
        compiler_params=pltpu.CompilerParams(
            collective_id=1, has_side_effects=True, vmem_limit_bytes=VMEM_LIMIT
        ),
        name="reduce_rows",
    )(dq, dk.reshape(PLANE, 2, D, B), dv.reshape(PLANE, 2, D, B))


def finish_kernel(dq_own, back, k_sum, v_sum, query_ref, key_ref, value_ref):
    scale = jnp.float32(D**-0.5)
    for blk in (0, 1):
        rows = slice(blk * B, (blk + 1) * B)
        for h in range(H):
            cols = slice(h * D, (h + 1) * D)
            query_ref[rows, cols] = (scale * (dq_own[blk, cols, :] + back[blk, cols, :].astype(F32))).astype(BF)
        key_ref[rows, :] = (scale * k_sum[blk]).T.astype(BF)
        value_ref[rows, :] = v_sum[blk].T.astype(BF)


def finish(*arrays):
    grad = jax.ShapeDtypeStruct((T, D), BF)
    return pl.pallas_call(
        finish_kernel,
        out_shape=(jax.ShapeDtypeStruct((T, H * D), BF), grad, grad),
        in_specs=[VM] * 4,
        out_specs=(VM,) * 3,
        compiler_params=pltpu.CompilerParams(vmem_limit_bytes=VMEM_LIMIT),
        name="finish",
    )(*arrays)


def local(queries, keys, values, outputs, out_grad, lse, block_order, doc_lengths):
    swap = [(i, i ^ 4) for i in range(2 * PLANE)]
    pair_lse = lax.ppermute(lse, "ctx", swap)
    pair_q = lax.ppermute(queries, "ctx", swap)
    pair_g = lax.ppermute(out_grad, "ctx", swap)
    ka, va, qa, ga, qt, gt, lc, dc, delta = gather(keys, values, queries, out_grad, outputs, lse)
    pair_delta = lax.ppermute(delta, "ctx", swap)
    k = ka.reshape(2 * PLANE, B, D)
    v = va.reshape(2 * PLANE, B, D)
    dq_own, dk, dv = attend(True, block_order, doc_lengths, qa, ga, qt, gt, lc, dc, k, v)
    dq_pair, dk, dv = attend(False, block_order, doc_lengths, pair_q, pair_g, pair_lse, pair_delta, k, v, dk, dv)
    back, k_sum, v_sum = reduce(dq_pair, dk, dv)
    return finish(dq_own, back, k_sum, v_sum)


def solution(mesh):
    rows = P(("dp", "ctx"), None)
    return jax.shard_map(
        local,
        mesh=mesh,
        in_specs=(rows, rows, rows, rows, rows, P(None, ("dp", "ctx")), P("dp"), P("dp")),
        out_specs=(rows, rows, rows),
        check_vma=False,
    )
```

```python
import functools

import jax
import jax.numpy as jnp
from jax import lax
from jax.experimental import pallas as pl
from jax.experimental.pallas import tpu as pltpu
from jax.sharding import PartitionSpec as P

BF = jnp.bfloat16
F32 = jnp.float32
I32 = jnp.int32
MESH = pl.DeviceIdType.MESH
VM = pl.BlockSpec(memory_space=pltpu.VMEM)
SM = pl.BlockSpec(memory_space=pltpu.SMEM)
ANY = pl.BlockSpec(memory_space=pl.ANY)

RING = 4
PLANE = RING * RING
T = 256
B = 128
H = 8
D = 128
VMEM_LIMIT = 32 * 2**20


def dot(a, b, ca, cb):
    return lax.dot_general(a, b, (((ca,), (cb,)), ((), ())), preferred_element_type=F32)


def stay(array):
    return pltpu.with_memory_space_constraint(array, pltpu.HBM)


def coords():
    me = lax.axis_index("ctx")
    return me // 8, (me // 4) % 2, me % 4


def ident(z, y, x):
    return {"ctx": z * 8 + y * 4 + x}


def step_of(v, d):
    return lax.rem(v + d, RING)


def greet_signal(z, y, x):
    barrier = pltpu.get_barrier_semaphore()
    others = [ident(z, y, step_of(x, d)) for d in (1, 2, 3)]
    others += [ident(step_of(z, d), y, x) for d in (1, 2, 3)]
    others.append(ident(z, 1 - y, x))
    for other in others:
        pl.semaphore_signal(barrier, inc=1, device_id=other, device_id_type=MESH)


def greet_wait():
    pl.semaphore_wait(pltpu.get_barrier_semaphore(), 7)


def pieces(whole):
    hi = whole.astype(BF)
    left = whole - hi.astype(F32)
    mid = left.astype(BF)
    return hi, mid, (left - mid.astype(F32)).astype(BF)


def pack_kernel(q_ref, g_ref, o_ref, lse_ref, packed, outs, lses, sems):
    copies = [
        pltpu.make_async_copy(g_ref, packed.at[pl.ds(T, T)], sems.at[0]),
        pltpu.make_async_copy(o_ref, outs, sems.at[1]),
        pltpu.make_async_copy(lse_ref, lses, sems.at[2]),
        pltpu.make_async_copy(q_ref, packed.at[pl.ds(0, T)], sems.at[3]),
    ]
    for copy in copies:
        copy.start()
    for copy in copies[:3]:
        copy.wait()
    ones = jnp.ones((8, D), BF)
    deltas = []
    for h in range(H):
        cols = slice(h * D, (h + 1) * D)
        prod = packed[T : 2 * T, cols].astype(F32) * outs[:, cols].astype(F32)
        hi = prod.astype(BF)
        lo = (prod - hi.astype(F32)).astype(BF)
        deltas.append((dot(ones, hi, 1, 1) + dot(ones, lo, 1, 1))[0:1, :])
    whole = jnp.concatenate([jnp.minimum(lses[...], 1e30)] + deltas, axis=0)
    for i, piece in enumerate(pieces(whole)):
        packed[2 * T :, i * T : (i + 1) * T] = piece
    packed[2 * T :, 3 * T :] = jnp.zeros((2 * H, T), BF)
    copies[3].wait()


def pack(queries, out_grad, outputs, lse):
    return pl.pallas_call(
        pack_kernel,
        out_shape=pltpu.VMEM((2 * T + 2 * H, H * D), BF),
        in_specs=[ANY] * 4,
        out_specs=VM,
        scratch_shapes=[
            pltpu.VMEM((T, H * D), BF),
            pltpu.VMEM((H, T), F32),
            pltpu.SemaphoreType.DMA((4,)),
        ],
        compiler_params=pltpu.CompilerParams(vmem_limit_bytes=VMEM_LIMIT),
        name="pack_rows",
    )(*[stay(t) for t in (queries, out_grad, outputs, lse)])


def widen(packed, lc, dc):
    which = lax.broadcasted_iota(I32, (6 * H, D), 0) % (2 * H)
    for blk in (0, 1):
        parts = [packed[2 * T :, i * T + blk * B : i * T + (blk + 1) * B] for i in range(3)]
        parts = jnp.concatenate(parts, axis=0)
        for h in range(2 * H):
            select = jnp.where(which == h, 1.0, 0.0).astype(BF)
            (lc, dc)[h // H][blk, h % H * D : (h % H + 1) * D, :] = dot(parts, select, 0, 0)


def turn(packed, qt, gt):
    for dst, first in ((qt, 0), (gt, T)):
        for blk in (0, 1):
            for h in range(H):
                cols = slice(h * D, (h + 1) * D)
                dst[blk, :, cols] = packed[first + blk * B : first + (blk + 1) * B, cols].T


def gather_kernel(
    k_ref, v_ref, packed, ka, va, qt, gt, lc, dc, own_sem, s1, r1, s2, r2, s3, r3,
):
    z, y, x = coords()
    here = z * RING + x
    greet_signal(z, y, x)
    own = []
    for a, (src, dst) in enumerate(((k_ref, ka), (v_ref, va))):
        copy = pltpu.make_async_copy(src, dst.at[here], own_sem.at[a])
        copy.start()
        own.append(copy)
    greet_wait()

    def send(src, dst, ssem, rsem, to):
        copy = pltpu.make_async_remote_copy(
            src_ref=src, dst_ref=dst, send_sem=ssem, recv_sem=rsem, device_id=to, device_id_type=MESH
        )
        copy.start()
        return copy

    srcs, alls = (k_ref, v_ref), (ka, va)

    def first_peer(a, d):
        return ident(z, y, step_of(x, d)) if a == 0 else ident(step_of(z, d), y, x)

    def second_peer(a, d):
        return first_peer(1 - a, d)

    def slot_from(a, s, t=0):
        if a == 0:
            return step_of(z, RING - t) * RING + step_of(x, RING - s)
        return step_of(z, RING - s) * RING + step_of(x, RING - t)

    first, second, third = {}, {}, {}

    def spread(a, s):
        src = srcs[a] if s == 0 else alls[a].at[slot_from(a, s)]
        dst = alls[a].at[here if s == 0 else slot_from(a, s)]
        for e in (1, 3):
            second[a, s, e] = send(src, dst, s2.at[a, s, e - 1], r2.at[a, s, e - 1], second_peer(a, e))

    for d in (1, 3, 2):
        for a in (0, 1):
            first[a, d] = send(srcs[a], alls[a].at[here], s1.at[a, d - 1], r1.at[a, d - 1], first_peer(a, d))
    for a in (0, 1):
        spread(a, 0)

    for s in (1, 3, 2):
        for a in (0, 1):
            first[a, s].wait_recv()
            spread(a, s)

    def relay(s):
        for e, half in ((1, 0), (3, 1)):
            for a in (0, 1):
                second[a, s, e].wait_recv()
                part = alls[a].at[slot_from(a, s, e), pl.ds(half * B, B)]
                third[a, s, half] = send(part, part, s3.at[a, s, half], r3.at[a, s, half], second_peer(a, e))

    relay(0)
    for copy in own:
        copy.wait()
    relay(1)
    widen(packed, lc, dc)
    relay(3)
    turn(packed, qt, gt)
    relay(2)
    for copy in third.values():
        copy.wait_recv()
    for copy in list(first.values()) + list(second.values()) + list(third.values()):
        copy.wait_send()


def gather(keys, values, packed):
    dma = pltpu.SemaphoreType.DMA
    return pl.pallas_call(
        gather_kernel,
        out_shape=(
            pltpu.VMEM((PLANE, T, D), BF),
            pltpu.VMEM((PLANE, T, D), BF),
            pltpu.VMEM((2, D, H * B), BF),
            pltpu.VMEM((2, D, H * B), BF),
            pltpu.VMEM((2, H * B, D), F32),
            pltpu.VMEM((2, H * B, D), F32),
        ),
        in_specs=[ANY] * 2 + [VM],
        out_specs=(VM,) * 6,
        scratch_shapes=[
            dma((2,)), dma((2, 3)), dma((2, 3)), dma((2, 4, 3)), dma((2, 4, 3)), dma((2, 4, 2)), dma((2, 4, 2)),
        ],
        compiler_params=pltpu.CompilerParams(
            collective_id=0, has_side_effects=True, vmem_limit_bytes=VMEM_LIMIT
        ),
        name="gather_rows",
    )(stay(keys), stay(values), packed)


KEYS = 36
NEVER = 1 << 20


def attend_kernel(own, order, lens, *refs):
    if own:
        packed, k_ref, v_ref, qt, gt, lc, dc, dqa, dk, dv = refs[:10]
        slots, places, qfrom, qbase, pbuf, dbuf = refs[10:]
    else:
        packed, k_ref, v_ref, _, _, dq_out, dk, dv = refs[:8]
        slots, places, qfrom, qbase, pbuf, dbuf, qt, gt, lc, dc, dqa = refs[8:]
    me = lax.axis_index("ctx")
    plane = (me // 4) % 2
    owner = me if own else me + 4 - 8 * plane

    ats = [order[owner * 2 + blk] for blk in (0, 1)]
    row = lax.broadcasted_iota(I32, (B, D), 0)
    lows = [jnp.int32(0), jnp.int32(0)]
    begins = [jnp.zeros_like(row), jnp.zeros_like(row)]
    end = jnp.int32(0)
    for d in range(lens.shape[0]):
        end = end + lens[d]
        for blk in (0, 1):
            lows[blk] = jnp.where(end <= ats[blk] * B, end, lows[blk])
            begins[blk] = jnp.where(end <= ats[blk] * B + row, end, begins[blk])
    lows = [low // B for low in lows]
    for blk in (0, 1):
        qfrom[blk] = begins[blk]
        qbase[blk] = ats[blk] * B

    def list_keys(i, counts):
        counts = list(counts)
        for j in range(8):
            slot = i * 8 + j
            p = order[i * 16 + plane * 8 + j]
            for blk in (0, 1):
                slots[blk * KEYS + counts[blk]] = slot
                places[blk * KEYS + counts[blk]] = p * B
                needed = (p >= lows[blk]) & (p <= ats[blk])
                counts[blk] = counts[blk] + needed.astype(I32)
        return tuple(counts)

    counts = lax.fori_loop(0, 4, list_keys, (jnp.int32(0), jnp.int32(0)))
    for blk in (0, 1):
        for i in range(3):
            slots[blk * KEYS + counts[blk] + i] = 0
            places[blk * KEYS + counts[blk] + i] = NEVER
    items = [(count + 1) // 2 for count in counts]
    total = items[0] + items[1]

    dqa[...] = jnp.zeros_like(dqa)
    if own:
        dk[...] = jnp.zeros_like(dk)
        dv[...] = jnp.zeros_like(dv)
    else:
        widen(packed, lc, dc)
        turn(packed, qt, gt)
    scale = jnp.float32(D**-0.5)
    across = lax.broadcasted_iota(I32, (1, B), 1)

    def load(n):
        later = (n >= items[0]).astype(I32)
        at = later * (KEYS - 2 * items[0]) + 2 * n
        a, b = slots[at], slots[at + 1]
        kk = jnp.concatenate([k_ref[a], k_ref[b]], axis=0)
        vv = jnp.concatenate([v_ref[a], v_ref[b]], axis=0)
        return later, a, b, kk, vv, places[at], places[at + 1]

    def scores(item, par):
        blk, _, _, kk, vv, place_a, place_b = item
        key_pos = jnp.concatenate([place_a + across, place_b + across], axis=1)
        here = qbase[blk] + row
        here = jnp.concatenate([here, here], axis=1)
        begin = qfrom[blk]
        begin = jnp.concatenate([begin, begin], axis=1)
        allowed = (key_pos <= here) & (key_pos >= begin)
        allowed = jnp.concatenate([allowed, allowed], axis=0)
        for two in range(4):
            cols = slice(two * 256, (two + 1) * 256)
            heads = [slice((2 * two + i) * D, (2 * two + i + 1) * D) for i in (0, 1)]
            q_rows = pl.ds(pl.multiple_of(blk * B, B), B)
            g_rows = pl.ds(pl.multiple_of(T + blk * B, B), B)
            score = dot(jnp.concatenate([packed[q_rows, c] for c in heads], axis=0), kk, 1, 1)
            dprob = dot(jnp.concatenate([packed[g_rows, c] for c in heads], axis=0), vv, 1, 1)
            less = lc[blk, cols, :]
            delta = dc[blk, cols, :]
            prob = jnp.where(allowed, jnp.exp(score * scale - jnp.concatenate([less, less], axis=1)), 0.0)
            pbuf[par, cols, :] = prob.astype(BF)
            dbuf[par, cols, :] = (prob * (dprob - jnp.concatenate([delta, delta], axis=1))).astype(BF)

    def grads(item, par):
        blk, a, b, kk = item[:4]
        dqa[blk] += jnp.dot(dbuf[par], kk, preferred_element_type=F32)
        dv_term = jnp.dot(gt[blk], pbuf[par], preferred_element_type=F32)
        dk_term = jnp.dot(qt[blk], dbuf[par], preferred_element_type=F32)
        dk[a] += dk_term[:, :B]
        dk[b] += dk_term[:, B:]
        dv[a] += dv_term[:, :B]
        dv[b] += dv_term[:, B:]

    def two(i, c):
        now = [load(2 * i), load(2 * i + 1)]
        for par in (0, 1):
            scores(now[par], par)
        for par in (0, 1):
            grads(now[par], par)
        return c

    lax.fori_loop(0, (total + 1) // 2, two, 0)
    if not own:
        dq_out[...] = dqa[...].astype(BF)


def attend(own, order, lens, *arrays):
    sums = pltpu.VMEM((2 * PLANE, D, B), F32)
    rows = pltpu.VMEM((2, H * B, D), F32)
    cols = pltpu.VMEM((2, D, H * B), BF)
    scratch = [
        pltpu.SMEM((2 * KEYS,), I32),
        pltpu.SMEM((2 * KEYS,), I32),
        pltpu.VMEM((2, B, D), I32),
        pltpu.SMEM((2,), I32),
        pltpu.VMEM((2, H * B, 2 * B), BF),
        pltpu.VMEM((2, H * B, 2 * B), BF),
    ]
    if not own:
        scratch += [cols, cols, rows, rows, rows]
    return pl.pallas_call(
        functools.partial(attend_kernel, own),
        out_shape=(pltpu.VMEM((2, H * B, D), F32 if own else BF), sums, sums),
        in_specs=[SM] * 2 + [VM] * len(arrays),
        out_specs=(VM,) * 3,
        scratch_shapes=scratch,
        input_output_aliases={} if own else {5: 1, 6: 2},
        compiler_params=pltpu.CompilerParams(vmem_limit_bytes=VMEM_LIMIT),
        name="attend_own" if own else "attend_pair",
    )(stay(order), stay(lens), *arrays)


def reduce_kernel(dq_ref, dk_ref, dv_ref, back, k_sum, v_sum, out1, in1, out2, in2, s1, r1, s2, r2, ps, pr):
    z, y, x = coords()
    greet_signal(z, y, x)
    srcs = (dk_ref, dv_ref)
    for a in (0, 1):
        out1[a] = srcs[a][...].astype(BF)
    greet_wait()

    def send(src, dst, ssem, rsem, to):
        copy = pltpu.make_async_remote_copy(
            src_ref=src, dst_ref=dst, send_sem=ssem, recv_sem=rsem, device_id=to, device_id_type=MESH
        )
        copy.start()
        return copy

    def first_peer(a, d):
        return ident(step_of(z, d), y, x) if a == 0 else ident(z, y, step_of(x, d))

    def second_peer(a, e):
        return first_peer(1 - a, e)

    def slot(a, d, e):
        if a == 0:
            return step_of(z, d) * RING + step_of(x, e)
        return step_of(z, e) * RING + step_of(x, d)

    first, second = {}, {}
    for e in (2, 1, 3, 0):
        for a in (0, 1):
            for d in (2, 1, 3):
                first[a, e, d] = send(
                    out1.at[a, slot(a, d, e)], in1.at[a, e, d - 1], s1.at[a, e, d - 1], r1.at[a, e, d - 1],
                    first_peer(a, d),
                )
    across = send(dq_ref, back, ps, pr, ident(z, 1 - y, x))
    sums = []
    for e in (2, 1, 3, 0):
        for a in (0, 1):
            total = srcs[a][slot(a, 0, e)]
            for d in (1, 2, 3):
                first[a, e, d].wait_recv()
                total = total + in1[a, e, d - 1].astype(F32)
            if e:
                out2[a, e - 1] = total.astype(BF)
                second[a, e] = send(out2.at[a, e - 1], in2.at[a, e - 1], s2.at[a, e - 1], r2.at[a, e - 1], second_peer(a, e))
            else:
                sums.append(total)
    for a, dst in ((0, k_sum), (1, v_sum)):
        total = sums[a]
        for e in (1, 2, 3):
            second[a, e].wait_recv()
            total = total + in2[a, e - 1].astype(F32)
        dst[...] = total
    across.wait()
    for copy in list(first.values()) + list(second.values()):
        copy.wait_send()


def reduce(dq, dk, dv):
    dma = pltpu.SemaphoreType.DMA
    return pl.pallas_call(
        reduce_kernel,
        out_shape=(
            pltpu.VMEM((2, H * B, D), BF),
            pltpu.VMEM((2, D, B), F32),
            pltpu.VMEM((2, D, B), F32),
        ),
        in_specs=[VM] * 3,
        out_specs=(VM,) * 3,
        scratch_shapes=[
            pltpu.VMEM((2, PLANE, 2, D, B), BF),
            pltpu.VMEM((2, 4, 3, 2, D, B), BF),
            pltpu.VMEM((2, 3, 2, D, B), BF),
            pltpu.VMEM((2, 3, 2, D, B), BF),
            dma((2, 4, 3)), dma((2, 4, 3)), dma((2, 3)), dma((2, 3)), dma, dma,
        ],
        compiler_params=pltpu.CompilerParams(
            collective_id=1, has_side_effects=True, vmem_limit_bytes=VMEM_LIMIT
        ),
        name="reduce_rows",
    )(dq, dk.reshape(PLANE, 2, D, B), dv.reshape(PLANE, 2, D, B))


def finish_kernel(dq_own, back, k_sum, v_sum, query_ref, key_ref, value_ref):
    scale = jnp.float32(D**-0.5)
    for blk in (0, 1):
        rows = slice(blk * B, (blk + 1) * B)
        for h in range(H):
            cols = slice(h * D, (h + 1) * D)
            query_ref[rows, cols] = (scale * (dq_own[blk, cols, :] + back[blk, cols, :].astype(F32))).astype(BF)
        key_ref[rows, :] = (scale * k_sum[blk]).T.astype(BF)
        value_ref[rows, :] = v_sum[blk].T.astype(BF)


def finish(*arrays):
    grad = jax.ShapeDtypeStruct((T, D), BF)
    return pl.pallas_call(
        finish_kernel,
        out_shape=(jax.ShapeDtypeStruct((T, H * D), BF), grad, grad),
        in_specs=[VM] * 4,
        out_specs=(VM,) * 3,
        compiler_params=pltpu.CompilerParams(vmem_limit_bytes=VMEM_LIMIT),
        name="finish",
    )(*arrays)


def local(queries, keys, values, outputs, out_grad, lse, block_order, doc_lengths):
    swap = [(i, i ^ 4) for i in range(2 * PLANE)]
    packed = pack(queries, out_grad, outputs, lse)
    other = lax.ppermute(packed, "ctx", swap)
    ka, va, qt, gt, lc, dc = gather(keys, values, packed)
    k = ka.reshape(2 * PLANE, B, D)
    v = va.reshape(2 * PLANE, B, D)
    dq_own, dk, dv = attend(True, block_order, doc_lengths, packed, k, v, qt, gt, lc, dc)
    dq_pair, dk, dv = attend(False, block_order, doc_lengths, other, k, v, dk, dv)
    back, k_sum, v_sum = reduce(dq_pair, dk, dv)
    return finish(dq_own, back, k_sum, v_sum)


def solution(mesh):
    rows = P(("dp", "ctx"), None)
    return jax.shard_map(
        local,
        mesh=mesh,
        in_specs=(rows, rows, rows, rows, rows, P(None, ("dp", "ctx")), P("dp"), P("dp")),
        out_specs=(rows, rows, rows),
        check_vma=False,
    )
```

```python
import functools
import math

import jax
import jax.numpy as jnp
from jax import lax
from jax.experimental import pallas as pl
from jax.experimental.pallas import tpu as pltpu
from jax.sharding import PartitionSpec as P

BF = jnp.bfloat16
F32 = jnp.float32
I32 = jnp.int32
MESH = pl.DeviceIdType.MESH
VM = pl.BlockSpec(memory_space=pltpu.VMEM)
SM = pl.BlockSpec(memory_space=pltpu.SMEM)
ANY = pl.BlockSpec(memory_space=pl.ANY)

RING = 4
PLANE = RING * RING
T = 256
B = 128
H = 8
D = 128
VMEM_LIMIT = 32 * 2**20
LOG2E = math.log2(math.e)


def dot(a, b, ca, cb):
    return lax.dot_general(a, b, (((ca,), (cb,)), ((), ())), preferred_element_type=F32)


def stay(array):
    return pltpu.with_memory_space_constraint(array, pltpu.HBM)


def coords():
    me = lax.axis_index("ctx")
    return me // 8, (me // 4) % 2, me % 4


def ident(z, y, x):
    return {"ctx": z * 8 + y * 4 + x}


def step_of(v, d):
    return lax.rem(v + d, RING)


def greet_signal(z, y, x):
    barrier = pltpu.get_barrier_semaphore()
    others = [ident(z, y, step_of(x, d)) for d in (1, 2, 3)]
    others += [ident(step_of(z, d), y, x) for d in (1, 2, 3)]
    others.append(ident(z, 1 - y, x))
    for other in others:
        pl.semaphore_signal(barrier, inc=1, device_id=other, device_id_type=MESH)


def greet_wait():
    pl.semaphore_wait(pltpu.get_barrier_semaphore(), 7)


def pieces(whole):
    hi = whole.astype(BF)
    left = whole - hi.astype(F32)
    mid = left.astype(BF)
    return hi, mid, (left - mid.astype(F32)).astype(BF)


def widen(stats, side, blk, lc, dc, to):
    which = lax.broadcasted_iota(I32, (6 * H, D), 0) % (2 * H)
    parts = [stats[side, :, i * T + blk * B : i * T + (blk + 1) * B] for i in range(3)]
    parts = jnp.concatenate(parts, axis=0)
    for h in range(2 * H):
        select = jnp.where(which == h, 1.0, 0.0).astype(BF)
        (lc, dc)[h // H][to, h % H * D : (h % H + 1) * D, :] = dot(parts, select, 0, 0)


def turn(rows, blk, qt, gt):
    for dst, first in ((qt, 0), (gt, B)):
        for h in range(H):
            cols = slice(h * D, (h + 1) * D)
            dst[blk, :, cols] = rows[blk, first : first + B, cols].T


def gather_kernel(
    k_ref, v_ref, q_ref, g_ref, o_ref, lse_ref, ka, va, rows, tail, stats, qt, gt, lc, dc, dk, dv,
    outs, lses, own_sem, s1, r1, s2, r2, s3, r3, ps, pr,
):
    z, y, x = coords()
    here = z * RING + x
    pair = ident(z, 1 - y, x)
    greet_signal(z, y, x)
    copies = []

    def keep(src, dst):
        copy = pltpu.make_async_copy(src, dst, own_sem.at[len(copies)])
        copy.start()
        copies.append(copy)

    first_rows, last_rows = pl.ds(0, B), pl.ds(B, B)
    keep(g_ref.at[first_rows], rows.at[0, last_rows])
    keep(g_ref.at[last_rows], rows.at[1, last_rows])
    keep(o_ref, outs)
    keep(lse_ref, lses)
    keep(q_ref.at[first_rows], rows.at[0, first_rows])
    keep(q_ref.at[last_rows], rows.at[1, first_rows])
    keep(q_ref.at[last_rows], tail.at[first_rows])
    keep(g_ref.at[last_rows], tail.at[last_rows])
    keep(k_ref, ka.at[here])
    keep(v_ref, va.at[here])
    greet_wait()

    def send(src, dst, ssem, rsem, to):
        copy = pltpu.make_async_remote_copy(
            src_ref=src, dst_ref=dst, send_sem=ssem, recv_sem=rsem, device_id=to, device_id_type=MESH
        )
        copy.start()
        return copy

    srcs, alls = (k_ref, v_ref), (ka, va)

    def first_peer(a, d):
        return ident(z, y, step_of(x, d)) if a == 0 else ident(step_of(z, d), y, x)

    def second_peer(a, d):
        return first_peer(1 - a, d)

    def slot_from(a, s, t=0):
        if a == 0:
            return step_of(z, RING - t) * RING + step_of(x, RING - s)
        return step_of(z, RING - s) * RING + step_of(x, RING - t)

    first, second, third = {}, {}, {}

    def spread(a, s):
        src = srcs[a] if s == 0 else alls[a].at[slot_from(a, s)]
        dst = alls[a].at[here if s == 0 else slot_from(a, s)]
        for e in (1, 3, 2) if s == 2 else (1, 3):
            second[a, s, e] = send(src, dst, s2.at[a, s, e - 1], r2.at[a, s, e - 1], second_peer(a, e))

    for d in (1, 3, 2):
        for a in (0, 1):
            first[a, d] = send(srcs[a], alls[a].at[here], s1.at[a, d - 1], r1.at[a, d - 1], first_peer(a, d))
    for a in (0, 1):
        spread(a, 0)
    across = [
        send(q_ref.at[first_rows], rows.at[2, first_rows], ps.at[0], pr.at[0], pair),
        send(g_ref.at[first_rows], rows.at[2, last_rows], ps.at[1], pr.at[1], pair),
    ]

    for copy in copies[:4]:
        copy.wait()
    ones = jnp.ones((8, D), BF)
    deltas = []
    for h in range(H):
        cols = slice(h * D, (h + 1) * D)
        grad = jnp.concatenate([rows[0, B:, cols], rows[1, B:, cols]], axis=0)
        prod = grad.astype(F32) * outs[:, cols].astype(F32)
        hi = prod.astype(BF)
        lo = (prod - hi.astype(F32)).astype(BF)
        deltas.append((dot(ones, hi, 1, 1) + dot(ones, lo, 1, 1))[0:1, :])
    whole = jnp.concatenate([jnp.minimum(lses[...], 1e30) * jnp.float32(LOG2E)] + deltas, axis=0)
    for i, piece in enumerate(pieces(whole)):
        stats[0, :, i * T : (i + 1) * T] = piece
    stats[0, :, 3 * T :] = jnp.zeros((2 * H, T), BF)
    across.append(send(stats.at[0], stats.at[1], ps.at[2], pr.at[2], pair))

    for s in (1, 3, 2):
        for a in (0, 1):
            first[a, s].wait_recv()
            spread(a, s)

    def relay(s):
        for e, half in ((1, 0), (3, 1)):
            for a in (0, 1):
                second[a, s, e].wait_recv()
                part = alls[a].at[slot_from(a, s, e), pl.ds(half * B, B)]
                third[a, s, half] = send(part, part, s3.at[a, s, half], r3.at[a, s, half], second_peer(a, e))

    dk[...] = jnp.zeros_like(dk)
    dv[...] = jnp.zeros_like(dv)
    relay(0)
    for copy in copies[4:]:
        copy.wait()
    relay(1)
    for blk in (0, 1):
        widen(stats, 0, blk, lc, dc, blk)
    relay(3)
    for blk in (0, 1):
        turn(rows, blk, qt, gt)
    for copy in across:
        copy.wait_recv()
    turn(rows, 2, qt, gt)
    widen(stats, 1, 0, lc, dc, 2)
    for a in (0, 1):
        for e in (1, 3, 2):
            second[a, 2, e].wait_recv()
    for copy in third.values():
        copy.wait_recv()
    for copy in list(first.values()) + list(second.values()) + list(third.values()) + across:
        copy.wait_send()


def gather(*arrays):
    dma = pltpu.SemaphoreType.DMA
    terms = pltpu.VMEM((3, H * B, D), F32)
    turned = pltpu.VMEM((3, D, H * B), BF)
    sums = pltpu.VMEM((2 * PLANE, D, B), F32)
    outs = (
        pltpu.VMEM((PLANE, T, D), BF),
        pltpu.VMEM((PLANE, T, D), BF),
        pltpu.VMEM((3, T, H * D), BF),
        pltpu.VMEM((T, H * D), BF),
        pltpu.VMEM((2, 2 * H, H * D), BF),
        turned, turned, terms, terms, sums, sums,
    )
    return pl.pallas_call(
        gather_kernel,
        out_shape=outs,
        in_specs=[ANY] * len(arrays),
        out_specs=(VM,) * len(outs),
        scratch_shapes=[
            pltpu.VMEM((T, H * D), BF),
            pltpu.VMEM((H, T), F32),
            dma((10,)), dma((2, 3)), dma((2, 3)), dma((2, 4, 3)), dma((2, 4, 3)),
            dma((2, 4, 2)), dma((2, 4, 2)), dma((3,)), dma((3,)),
        ],
        compiler_params=pltpu.CompilerParams(
            collective_id=0, has_side_effects=True, vmem_limit_bytes=VMEM_LIMIT
        ),
        name="gather_rows",
    )(*[stay(t) for t in arrays])


KEYS = 36
NEVER = 1 << 20


def attend_kernel(count, order, lens, *refs):
    early = count == 3
    if early:
        k_ref, v_ref, rows, qt, gt, lc, dc, _, _, dk, dv, dqa, dq_out = refs[:13]
        slots, places, qfrom, qbase, pbuf, dbuf = refs[13:]
    else:
        k_ref, v_ref, rows, stats, _, _, dk, dv, dq_out = refs[:9]
        slots, places, qfrom, qbase, pbuf, dbuf, qt, gt, lc, dc, dqa = refs[9:]
    me = lax.axis_index("ctx")
    plane = (me // 4) % 2
    mate = me + 4 - 8 * plane
    blocks = range(count)

    ats = [order[i] for i in ((me * 2, me * 2 + 1, mate * 2) if early else (mate * 2 + 1,))]
    row = lax.broadcasted_iota(I32, (B, D), 0)
    lows = [jnp.int32(0) for _ in blocks]
    begins = [jnp.zeros_like(row) for _ in blocks]
    end = jnp.int32(0)
    for d in range(lens.shape[0]):
        end = end + lens[d]
        for blk in blocks:
            lows[blk] = jnp.where(end <= ats[blk] * B, end, lows[blk])
            begins[blk] = jnp.where(end <= ats[blk] * B + row, end, begins[blk])
    lows = [low // B for low in lows]
    for blk in blocks:
        qfrom[blk] = begins[blk]
        qbase[blk] = ats[blk] * B

    def list_keys(i, counts):
        counts = list(counts)
        for j in range(8):
            slot = i * 8 + j
            p = order[i * 16 + plane * 8 + j]
            for blk in blocks:
                slots[blk * KEYS + counts[blk]] = slot
                places[blk * KEYS + counts[blk]] = p * B
                needed = (p >= lows[blk]) & (p <= ats[blk])
                counts[blk] = counts[blk] + needed.astype(I32)
        return tuple(counts)

    counts = lax.fori_loop(0, 4, list_keys, tuple(jnp.int32(0) for _ in blocks))
    for blk in blocks:
        slots[blk * KEYS + counts[blk]] = 0
        places[blk * KEYS + counts[blk]] = NEVER
    items = [(n + 1) // 2 for n in counts]
    total = sum(items[1:], items[0])

    dqa[...] = jnp.zeros_like(dqa)
    if not early:
        widen(stats, 1, 1, lc, dc, 0)
        turn(rows, 0, qt, gt)
    scale = jnp.float32(D**-0.5 * LOG2E)
    across = lax.broadcasted_iota(I32, (1, B), 1)

    def load(n):
        at, which, past = 2 * n, jnp.int32(0), jnp.int32(0)
        for blk in blocks[:-1]:
            past = past + items[blk]
            later = n >= past
            which = which + later.astype(I32)
            at = at + jnp.where(later, KEYS - 2 * items[blk], 0)
        a, b = slots[at], slots[at + 1]
        kk = jnp.concatenate([k_ref[a], k_ref[b]], axis=0)
        vv = jnp.concatenate([v_ref[a], v_ref[b]], axis=0)
        return which, a, b, kk, vv, places[at], places[at + 1]

    def scores(item, par):
        blk, _, _, kk, vv, place_a, place_b = item
        key_pos = jnp.concatenate([place_a + across, place_b + across], axis=1)
        here = qbase[blk] + row
        here = jnp.concatenate([here, here], axis=1)
        begin = qfrom[blk]
        begin = jnp.concatenate([begin, begin], axis=1)
        allowed = (key_pos <= here) & (key_pos >= begin)
        allowed = jnp.concatenate([allowed, allowed], axis=0)
        for two in range(4):
            cols = slice(two * 256, (two + 1) * 256)
            heads = [slice((2 * two + i) * D, (2 * two + i + 1) * D) for i in (0, 1)]
            score = dot(jnp.concatenate([rows[blk, :B, c] for c in heads], axis=0), kk, 1, 1)
            dprob = dot(jnp.concatenate([rows[blk, B:, c] for c in heads], axis=0), vv, 1, 1)
            less = lc[blk, cols, :]
            delta = dc[blk, cols, :]
            prob = jnp.where(allowed, jnp.exp2(score * scale - jnp.concatenate([less, less], axis=1)), 0.0)
            pbuf[par, cols, :] = prob.astype(BF)
            dbuf[par, cols, :] = (prob * (dprob - jnp.concatenate([delta, delta], axis=1))).astype(BF)

    def grads(item, par):
        blk, a, b, kk = item[:4]
        dqa[blk] += jnp.dot(dbuf[par], kk, preferred_element_type=F32)
        dv_term = jnp.dot(gt[blk], pbuf[par], preferred_element_type=F32)
        dk_term = jnp.dot(qt[blk], dbuf[par], preferred_element_type=F32)
        dk[a] += dk_term[:, :B]
        dk[b] += dk_term[:, B:]
        dv[a] += dv_term[:, :B]
        dv[b] += dv_term[:, B:]

    def two(i, c):
        now = [load(2 * i), load(2 * i + 1)]
        for par in (0, 1):
            scores(now[par], par)
        for par in (0, 1):
            grads(now[par], par)
        return c

    lax.fori_loop(0, total // 2, two, 0)

    @pl.when(total % 2 == 1)
    def _():
        last = load(total - 1)
        scores(last, 0)
        grads(last, 0)

    dq_out[...] = dqa[count - 1].astype(BF)


def attend(count, order, lens, *arrays):
    sums = pltpu.VMEM((2 * PLANE, D, B), F32)
    terms = pltpu.VMEM((count, H * B, D), F32)
    turned = pltpu.VMEM((count, D, H * B), BF)
    part = pltpu.VMEM((H * B, D), BF)
    scratch = [
        pltpu.SMEM((count * KEYS,), I32),
        pltpu.SMEM((count * KEYS,), I32),
        pltpu.VMEM((count, B, D), I32),
        pltpu.SMEM((count,), I32),
        pltpu.VMEM((2, H * B, 2 * B), BF),
        pltpu.VMEM((2, H * B, 2 * B), BF),
    ]
    if count == 3:
        outs = (sums, sums, terms, part)
    else:
        scratch += [turned, turned, terms, terms, terms]
        outs = (sums, sums, part)
    return pl.pallas_call(
        functools.partial(attend_kernel, count),
        out_shape=outs,
        in_specs=[SM] * 2 + [VM] * len(arrays),
        out_specs=(VM,) * len(outs),
        scratch_shapes=scratch,
        input_output_aliases={len(arrays): 0, len(arrays) + 1: 1},
        compiler_params=pltpu.CompilerParams(vmem_limit_bytes=VMEM_LIMIT),
        name="attend_early" if count == 3 else "attend_late",
    )(stay(order), stay(lens), *arrays)


def reduce_kernel(dq_early, dq_late, dk_ref, dv_ref, back, k_sum, v_sum, out1, in1, out_joint, in_side, out2, in2, s1, r1, s2, r2, ps, pr):
    z, y, x = coords()
    greet_signal(z, y, x)
    srcs = (dk_ref, dv_ref)
    for a in (0, 1):
        out1[a] = srcs[a][...].astype(BF)
    greet_wait()

    def send(src, dst, ssem, rsem, to):
        copy = pltpu.make_async_remote_copy(
            src_ref=src, dst_ref=dst, send_sem=ssem, recv_sem=rsem, device_id=to, device_id_type=MESH
        )
        copy.start()
        return copy

    def first_peer(a, d):
        return ident(step_of(z, d), y, x) if a == 0 else ident(z, y, step_of(x, d))

    def second_peer(a, e):
        return first_peer(1 - a, e)

    def slot(a, d, e):
        if a == 0:
            return step_of(z, d) * RING + step_of(x, e)
        return step_of(z, e) * RING + step_of(x, d)

    order, sides = (2, 1, 3, 0), ((1, 0), (3, 1))
    far, plain, joint, second = {}, {}, {}, {}
    for e in order:
        for a in (0, 1):
            for d, half in sides:
                far[a, e, half] = send(
                    out1.at[a, slot(a, 2, e), half], in1.at[a, e, half], s1.at[a, e, half], r1.at[a, e, half],
                    first_peer(a, d),
                )
    across = [
        send(src, back.at[blk], ps.at[blk], pr.at[blk], ident(z, 1 - y, x))
        for blk, src in enumerate((dq_early, dq_late))
    ]
    for e in order:
        for a in (0, 1):
            for d, half in sides:
                plain[a, e, half] = send(
                    out1.at[a, slot(a, d, e), 1 - half], in_side.at[a, e, half, 1 - half],
                    s1.at[a, e, 2 + half], r1.at[a, e, 2 + half], first_peer(a, d),
                )
        for a in (0, 1):
            for d, half in sides:
                far[a, e, half].wait_recv()
                both = srcs[a][slot(a, d, e), half] + in1[a, e, half].astype(F32)
                out_joint[a, e, half] = both.astype(BF)
                joint[a, e, half] = send(
                    out_joint.at[a, e, half], in_side.at[a, e, half, half],
                    s1.at[a, e, 4 + half], r1.at[a, e, 4 + half], first_peer(a, d),
                )
    sums = []
    for e in order:
        for a in (0, 1):
            for half in (0, 1):
                plain[a, e, half].wait_recv()
                joint[a, e, half].wait_recv()
            total = srcs[a][slot(a, 0, e)] + in_side[a, e, 0].astype(F32) + in_side[a, e, 1].astype(F32)
            if e:
                out2[a, e - 1] = total.astype(BF)
                second[a, e] = send(out2.at[a, e - 1], in2.at[a, e - 1], s2.at[a, e - 1], r2.at[a, e - 1], second_peer(a, e))
            else:
                sums.append(total)
    for a, dst in ((0, k_sum), (1, v_sum)):
        total = sums[a]
        for e in (1, 2, 3):
            second[a, e].wait_recv()
            total = total + in2[a, e - 1].astype(F32)
        dst[...] = total
    for copy in across:
        copy.wait()
    for copy in [*far.values(), *plain.values(), *joint.values(), *second.values()]:
        copy.wait_send()


def reduce(dq_early, dq_late, dk, dv):
    dma = pltpu.SemaphoreType.DMA
    return pl.pallas_call(
        reduce_kernel,
        out_shape=(
            pltpu.VMEM((2, H * B, D), BF),
            pltpu.VMEM((2, D, B), F32),
            pltpu.VMEM((2, D, B), F32),
        ),
        in_specs=[VM] * 4,
        out_specs=(VM,) * 3,
        scratch_shapes=[
            pltpu.VMEM((2, PLANE, 2, D, B), BF),
            pltpu.VMEM((2, 4, 2, D, B), BF),
            pltpu.VMEM((2, 4, 2, D, B), BF),
            pltpu.VMEM((2, 4, 2, 2, D, B), BF),
            pltpu.VMEM((2, 3, 2, D, B), BF),
            pltpu.VMEM((2, 3, 2, D, B), BF),
            dma((2, 4, 6)), dma((2, 4, 6)), dma((2, 3)), dma((2, 3)), dma((2,)), dma((2,)),
        ],
        compiler_params=pltpu.CompilerParams(
            collective_id=1, has_side_effects=True, vmem_limit_bytes=VMEM_LIMIT
        ),
        name="reduce_rows",
    )(dq_early, dq_late, dk.reshape(PLANE, 2, D, B), dv.reshape(PLANE, 2, D, B))


def finish_kernel(dq_own, back, k_sum, v_sum, query_ref, key_ref, value_ref):
    scale = jnp.float32(D**-0.5)
    for blk in (0, 1):
        rows = slice(blk * B, (blk + 1) * B)
        for h in range(H):
            cols = slice(h * D, (h + 1) * D)
            query_ref[rows, cols] = (scale * (dq_own[blk, cols, :] + back[blk, cols, :].astype(F32))).astype(BF)
        key_ref[rows, :] = (scale * k_sum[blk]).T.astype(BF)
        value_ref[rows, :] = v_sum[blk].T.astype(BF)


def finish(*arrays):
    grad = jax.ShapeDtypeStruct((T, D), BF)
    return pl.pallas_call(
        finish_kernel,
        out_shape=(jax.ShapeDtypeStruct((T, H * D), BF), grad, grad),
        in_specs=[VM] * 4,
        out_specs=(VM,) * 3,
        compiler_params=pltpu.CompilerParams(vmem_limit_bytes=VMEM_LIMIT),
        name="finish",
    )(*arrays)


def local(queries, keys, values, outputs, out_grad, lse, block_order, doc_lengths):
    swap = [(i, i ^ 4) for i in range(2 * PLANE)]
    ka, va, rows, tail, stats, qt, gt, lc, dc, dk, dv = gather(keys, values, queries, out_grad, outputs, lse)
    pair_tail = lax.ppermute(tail, "ctx", swap)
    k = ka.reshape(2 * PLANE, B, D)
    v = va.reshape(2 * PLANE, B, D)
    dk, dv, dq_own, dq_early = attend(3, block_order, doc_lengths, k, v, rows, qt, gt, lc, dc, dk, dv)
    pair_rows = pair_tail.reshape(1, T, H * D)
    dk, dv, dq_late = attend(1, block_order, doc_lengths, k, v, pair_rows, stats, dk, dv)
    back, k_sum, v_sum = reduce(dq_early, dq_late, dk, dv)
    return finish(dq_own, back, k_sum, v_sum)


def solution(mesh):
    rows = P(("dp", "ctx"), None)
    return jax.shard_map(
        local,
        mesh=mesh,
        in_specs=(rows, rows, rows, rows, rows, P(None, ("dp", "ctx")), P("dp"), P("dp")),
        out_specs=(rows, rows, rows),
        check_vma=False,
    )
```

```python
import functools
import math

import jax
import jax.numpy as jnp
from jax import lax
from jax.experimental import pallas as pl
from jax.experimental.pallas import tpu as pltpu
from jax.sharding import PartitionSpec as P

BF = jnp.bfloat16
F32 = jnp.float32
I32 = jnp.int32
MESH = pl.DeviceIdType.MESH
VM = pl.BlockSpec(memory_space=pltpu.VMEM)
SM = pl.BlockSpec(memory_space=pltpu.SMEM)
ANY = pl.BlockSpec(memory_space=pl.ANY)

RING = 4
PLANE = RING * RING
T = 256
B = 128
H = 8
D = 128
VMEM_LIMIT = 32 * 2**20
LOG2E = math.log2(math.e)


def dot(a, b, ca, cb):
    return lax.dot_general(a, b, (((ca,), (cb,)), ((), ())), preferred_element_type=F32)


def stay(array):
    return pltpu.with_memory_space_constraint(array, pltpu.HBM)


def coords():
    me = lax.axis_index("ctx")
    return me // 8, (me // 4) % 2, me % 4


def ident(z, y, x):
    return {"ctx": z * 8 + y * 4 + x}


def step_of(v, d):
    return lax.rem(v + d, RING)


def greet_signal(z, y, x):
    barrier = pltpu.get_barrier_semaphore()
    others = [ident(z, y, step_of(x, d)) for d in (1, 2, 3)]
    others += [ident(step_of(z, d), y, x) for d in (1, 2, 3)]
    others.append(ident(z, 1 - y, x))
    for other in others:
        pl.semaphore_signal(barrier, inc=1, device_id=other, device_id_type=MESH)


def greet_wait():
    pl.semaphore_wait(pltpu.get_barrier_semaphore(), 7)


def pieces(whole):
    hi = whole.astype(BF)
    left = whole - hi.astype(F32)
    mid = left.astype(BF)
    return hi, mid, (left - mid.astype(F32)).astype(BF)


def widen(stats, side, blk, lc, dc, to):
    which = lax.broadcasted_iota(I32, (6 * H, D), 0) % (2 * H)
    parts = [stats[side, :, i * T + blk * B : i * T + (blk + 1) * B] for i in range(3)]
    parts = jnp.concatenate(parts, axis=0)
    for h in range(2 * H):
        select = jnp.where(which == h, 1.0, 0.0).astype(BF)
        (lc, dc)[h // H][to, h % H * D : (h % H + 1) * D, :] = dot(parts, select, 0, 0)


def turn(rows, blk, qt, gt):
    for dst, first in ((qt, 0), (gt, B)):
        for h in range(H):
            cols = slice(h * D, (h + 1) * D)
            dst[blk, :, cols] = rows[blk, first : first + B, cols].T


def gather_kernel(
    k_ref, v_ref, q_ref, g_ref, o_ref, lse_ref, ka, va, rows, tail, stats, qt, gt, lc, dc, dk, dv,
    outs, lses, own_sem, s1, r1, s2, r2, s3, r3, ps, pr,
):
    z, y, x = coords()
    here = z * RING + x
    pair = ident(z, 1 - y, x)
    greet_signal(z, y, x)
    copies = []

    def keep(src, dst):
        copy = pltpu.make_async_copy(src, dst, own_sem.at[len(copies)])
        copy.start()
        copies.append(copy)

    first_rows, last_rows = pl.ds(0, B), pl.ds(B, B)
    keep(g_ref.at[first_rows], rows.at[0, last_rows])
    keep(g_ref.at[last_rows], rows.at[1, last_rows])
    keep(o_ref, outs)
    keep(lse_ref, lses)
    keep(q_ref.at[first_rows], rows.at[0, first_rows])
    keep(q_ref.at[last_rows], rows.at[1, first_rows])
    keep(q_ref.at[last_rows], tail.at[first_rows])
    keep(g_ref.at[last_rows], tail.at[last_rows])
    keep(k_ref, ka.at[here])
    keep(v_ref, va.at[here])
    greet_wait()

    def send(src, dst, ssem, rsem, to):
        copy = pltpu.make_async_remote_copy(
            src_ref=src, dst_ref=dst, send_sem=ssem, recv_sem=rsem, device_id=to, device_id_type=MESH
        )
        copy.start()
        return copy

    srcs, alls = (k_ref, v_ref), (ka, va)

    def first_peer(a, d):
        return ident(z, y, step_of(x, d)) if a == 0 else ident(step_of(z, d), y, x)

    def second_peer(a, d):
        return first_peer(1 - a, d)

    def slot_from(a, s, t=0):
        if a == 0:
            return step_of(z, RING - t) * RING + step_of(x, RING - s)
        return step_of(z, RING - s) * RING + step_of(x, RING - t)

    first, second, third = {}, {}, {}

    def spread(a, s):
        src = srcs[a] if s == 0 else alls[a].at[slot_from(a, s)]
        dst = alls[a].at[here if s == 0 else slot_from(a, s)]
        for e in (1, 3, 2) if s == 2 else (1, 3):
            second[a, s, e] = send(src, dst, s2.at[a, s, e - 1], r2.at[a, s, e - 1], second_peer(a, e))

    for d in (1, 3, 2):
        for a in (0, 1):
            first[a, d] = send(srcs[a], alls[a].at[here], s1.at[a, d - 1], r1.at[a, d - 1], first_peer(a, d))
    for a in (0, 1):
        spread(a, 0)
    across = [
        send(q_ref.at[first_rows], rows.at[2, first_rows], ps.at[0], pr.at[0], pair),
        send(g_ref.at[first_rows], rows.at[2, last_rows], ps.at[1], pr.at[1], pair),
    ]

    for copy in copies[:4]:
        copy.wait()
    ones = jnp.ones((8, D), BF)
    deltas = []
    for h in range(H):
        cols = slice(h * D, (h + 1) * D)
        grad = jnp.concatenate([rows[0, B:, cols], rows[1, B:, cols]], axis=0)
        prod = grad.astype(F32) * outs[:, cols].astype(F32)
        hi = prod.astype(BF)
        lo = (prod - hi.astype(F32)).astype(BF)
        deltas.append((dot(ones, hi, 1, 1) + dot(ones, lo, 1, 1))[0:1, :])
    whole = jnp.concatenate([jnp.minimum(lses[...], 1e30) * jnp.float32(LOG2E)] + deltas, axis=0)
    for i, piece in enumerate(pieces(whole)):
        stats[0, :, i * T : (i + 1) * T] = piece
    stats[0, :, 3 * T :] = jnp.zeros((2 * H, T), BF)
    across.append(send(stats.at[0], stats.at[1], ps.at[2], pr.at[2], pair))

    def forward(s):
        for a in (0, 1):
            first[a, s].wait_recv()
            spread(a, s)

    forward(1)
    forward(3)
    forward(2)
    dk[...] = jnp.zeros_like(dk)
    dv[...] = jnp.zeros_like(dv)
    for copy in copies[4:]:
        copy.wait()
    for blk in (0, 1):
        widen(stats, 0, blk, lc, dc, blk)
        turn(rows, blk, qt, gt)

    def relay(s):
        for e, half in ((1, 0), (3, 1)):
            for a in (0, 1):
                second[a, s, e].wait_recv()
                part = alls[a].at[slot_from(a, s, e), pl.ds(half * B, B)]
                third[a, s, half] = send(part, part, s3.at[a, s, half], r3.at[a, s, half], second_peer(a, e))

    relay(0)
    relay(1)
    relay(3)
    for copy in across:
        copy.wait_recv()
    turn(rows, 2, qt, gt)
    widen(stats, 1, 0, lc, dc, 2)
    for a in (0, 1):
        for e in (1, 3, 2):
            second[a, 2, e].wait_recv()
    for copy in third.values():
        copy.wait_recv()
    for copy in list(first.values()) + list(second.values()) + list(third.values()) + across:
        copy.wait_send()


def gather(*arrays):
    dma = pltpu.SemaphoreType.DMA
    terms = pltpu.VMEM((3, H * B, D), F32)
    turned = pltpu.VMEM((3, D, H * B), BF)
    sums = pltpu.VMEM((2 * PLANE, D, B), F32)
    outs = (
        pltpu.VMEM((PLANE, T, D), BF),
        pltpu.VMEM((PLANE, T, D), BF),
        pltpu.VMEM((3, T, H * D), BF),
        pltpu.VMEM((T, H * D), BF),
        pltpu.VMEM((2, 2 * H, H * D), BF),
        turned, turned, terms, terms, sums, sums,
    )
    return pl.pallas_call(
        gather_kernel,
        out_shape=outs,
        in_specs=[ANY] * len(arrays),
        out_specs=(VM,) * len(outs),
        scratch_shapes=[
            pltpu.VMEM((T, H * D), BF),
            pltpu.VMEM((H, T), F32),
            dma((10,)), dma((2, 3)), dma((2, 3)), dma((2, 4, 3)), dma((2, 4, 3)),
            dma((2, 4, 2)), dma((2, 4, 2)), dma((3,)), dma((3,)),
        ],
        compiler_params=pltpu.CompilerParams(
            collective_id=0, has_side_effects=True, vmem_limit_bytes=VMEM_LIMIT
        ),
        name="gather_rows",
    )(*[stay(t) for t in arrays])


KEYS = 36
NEVER = 1 << 20


def attend_kernel(count, order, lens, *refs):
    early = count == 3
    if early:
        k_ref, v_ref, rows, qt, gt, lc, dc, _, _, dk, dv, dqa, dq_out = refs[:13]
        slots, places, qfrom, qbase, pbuf, dbuf = refs[13:]
    else:
        k_ref, v_ref, rows, stats, _, _, dk, dv, dq_out = refs[:9]
        slots, places, qfrom, qbase, pbuf, dbuf, qt, gt, lc, dc, dqa = refs[9:]
    me = lax.axis_index("ctx")
    plane = (me // 4) % 2
    mate = me + 4 - 8 * plane
    blocks = range(count)

    ats = [order[i] for i in ((me * 2, me * 2 + 1, mate * 2) if early else (mate * 2 + 1,))]
    row = lax.broadcasted_iota(I32, (B, D), 0)
    lows = [jnp.int32(0) for _ in blocks]
    begins = [jnp.zeros_like(row) for _ in blocks]
    end = jnp.int32(0)
    for d in range(lens.shape[0]):
        end = end + lens[d]
        for blk in blocks:
            lows[blk] = jnp.where(end <= ats[blk] * B, end, lows[blk])
            begins[blk] = jnp.where(end <= ats[blk] * B + row, end, begins[blk])
    lows = [low // B for low in lows]
    for blk in blocks:
        qfrom[blk] = begins[blk]
        qbase[blk] = ats[blk] * B

    def list_keys(i, counts):
        counts = list(counts)
        for j in range(8):
            slot = i * 8 + j
            p = order[i * 16 + plane * 8 + j]
            for blk in blocks:
                slots[blk * KEYS + counts[blk]] = slot
                places[blk * KEYS + counts[blk]] = p * B
                needed = (p >= lows[blk]) & (p <= ats[blk])
                counts[blk] = counts[blk] + needed.astype(I32)
        return tuple(counts)

    counts = lax.fori_loop(0, 4, list_keys, tuple(jnp.int32(0) for _ in blocks))
    for blk in blocks:
        slots[blk * KEYS + counts[blk]] = 0
        places[blk * KEYS + counts[blk]] = NEVER
    items = [(n + 1) // 2 for n in counts]
    total = sum(items[1:], items[0])

    dqa[...] = jnp.zeros_like(dqa)
    if not early:
        widen(stats, 1, 1, lc, dc, 0)
        turn(rows, 0, qt, gt)
    scale = jnp.float32(D**-0.5 * LOG2E)
    across = lax.broadcasted_iota(I32, (1, B), 1)

    def load(n):
        at, which, past = 2 * n, jnp.int32(0), jnp.int32(0)
        for blk in blocks[:-1]:
            past = past + items[blk]
            later = n >= past
            which = which + later.astype(I32)
            at = at + jnp.where(later, KEYS - 2 * items[blk], 0)
        a, b = slots[at], slots[at + 1]
        kk = jnp.concatenate([k_ref[a], k_ref[b]], axis=0)
        vv = jnp.concatenate([v_ref[a], v_ref[b]], axis=0)
        return which, a, b, kk, vv, places[at], places[at + 1]

    def scores(item, par):
        blk, _, _, kk, vv, place_a, place_b = item
        key_pos = jnp.concatenate([place_a + across, place_b + across], axis=1)
        here = qbase[blk] + row
        here = jnp.concatenate([here, here], axis=1)
        begin = qfrom[blk]
        begin = jnp.concatenate([begin, begin], axis=1)
        allowed = (key_pos <= here) & (key_pos >= begin)
        allowed = jnp.concatenate([allowed, allowed], axis=0)
        for two in range(4):
            cols = slice(two * 256, (two + 1) * 256)
            heads = [slice((2 * two + i) * D, (2 * two + i + 1) * D) for i in (0, 1)]
            score = dot(jnp.concatenate([rows[blk, :B, c] for c in heads], axis=0), kk, 1, 1)
            dprob = dot(jnp.concatenate([rows[blk, B:, c] for c in heads], axis=0), vv, 1, 1)
            less = lc[blk, cols, :]
            delta = dc[blk, cols, :]
            prob = jnp.where(allowed, jnp.exp2(score * scale - jnp.concatenate([less, less], axis=1)), 0.0)
            pbuf[par, cols, :] = prob.astype(BF)
            dbuf[par, cols, :] = (prob * (dprob - jnp.concatenate([delta, delta], axis=1))).astype(BF)

    def grads(item, par):
        blk, a, b, kk = item[:4]
        dqa[blk] += jnp.dot(dbuf[par], kk, preferred_element_type=F32)
        dv_term = jnp.dot(gt[blk], pbuf[par], preferred_element_type=F32)
        dk_term = jnp.dot(qt[blk], dbuf[par], preferred_element_type=F32)
        dk[a] += dk_term[:, :B]
        dk[b] += dk_term[:, B:]
        dv[a] += dv_term[:, :B]
        dv[b] += dv_term[:, B:]

    def two(i, c):
        now = [load(2 * i), load(2 * i + 1)]
        for par in (0, 1):
            scores(now[par], par)
        for par in (0, 1):
            grads(now[par], par)
        return c

    lax.fori_loop(0, total // 2, two, 0)

    @pl.when(total % 2 == 1)
    def _():
        last = load(total - 1)
        scores(last, 0)
        grads(last, 0)

    dq_out[...] = dqa[count - 1].astype(BF)


def attend(count, order, lens, *arrays):
    sums = pltpu.VMEM((2 * PLANE, D, B), F32)
    terms = pltpu.VMEM((count, H * B, D), F32)
    turned = pltpu.VMEM((count, D, H * B), BF)
    part = pltpu.VMEM((H * B, D), BF)
    scratch = [
        pltpu.SMEM((count * KEYS,), I32),
        pltpu.SMEM((count * KEYS,), I32),
        pltpu.VMEM((count, B, D), I32),
        pltpu.SMEM((count,), I32),
        pltpu.VMEM((2, H * B, 2 * B), BF),
        pltpu.VMEM((2, H * B, 2 * B), BF),
    ]
    if count == 3:
        outs = (sums, sums, terms, part)
    else:
        scratch += [turned, turned, terms, terms, terms]
        outs = (sums, sums, part)
    return pl.pallas_call(
        functools.partial(attend_kernel, count),
        out_shape=outs,
        in_specs=[SM] * 2 + [VM] * len(arrays),
        out_specs=(VM,) * len(outs),
        scratch_shapes=scratch,
        input_output_aliases={len(arrays): 0, len(arrays) + 1: 1},
        compiler_params=pltpu.CompilerParams(vmem_limit_bytes=VMEM_LIMIT),
        name="attend_early" if count == 3 else "attend_late",
    )(stay(order), stay(lens), *arrays)


def reduce_kernel(dq_early, dq_late, dk_ref, dv_ref, back, k_sum, v_sum, out1, in1, out_joint, in_side, out2, in2, s1, r1, s2, r2, ps, pr):
    z, y, x = coords()
    greet_signal(z, y, x)
    srcs = (dk_ref, dv_ref)
    for a in (0, 1):
        out1[a] = srcs[a][...].astype(BF)
    greet_wait()

    def send(src, dst, ssem, rsem, to):
        copy = pltpu.make_async_remote_copy(
            src_ref=src, dst_ref=dst, send_sem=ssem, recv_sem=rsem, device_id=to, device_id_type=MESH
        )
        copy.start()
        return copy

    def first_peer(a, d):
        return ident(step_of(z, d), y, x) if a == 0 else ident(z, y, step_of(x, d))

    def second_peer(a, e):
        return first_peer(1 - a, e)

    def slot(a, d, e):
        if a == 0:
            return step_of(z, d) * RING + step_of(x, e)
        return step_of(z, e) * RING + step_of(x, d)

    order, sides = (2, 1, 3, 0), ((1, 0), (3, 1))
    far, plain, joint, second = {}, {}, {}, {}
    for e in order:
        for a in (0, 1):
            for d, half in sides:
                far[a, e, half] = send(
                    out1.at[a, slot(a, 2, e), half], in1.at[a, e, half], s1.at[a, e, half], r1.at[a, e, half],
                    first_peer(a, d),
                )
    across = [
        send(src, back.at[blk], ps.at[blk], pr.at[blk], ident(z, 1 - y, x))
        for blk, src in enumerate((dq_early, dq_late))
    ]
    for e in order:
        for a in (0, 1):
            for d, half in sides:
                plain[a, e, half] = send(
                    out1.at[a, slot(a, d, e), 1 - half], in_side.at[a, e, half, 1 - half],
                    s1.at[a, e, 2 + half], r1.at[a, e, 2 + half], first_peer(a, d),
                )
        for a in (0, 1):
            for d, half in sides:
                far[a, e, half].wait_recv()
                both = srcs[a][slot(a, d, e), half] + in1[a, e, half].astype(F32)
                out_joint[a, e, half] = both.astype(BF)
                joint[a, e, half] = send(
                    out_joint.at[a, e, half], in_side.at[a, e, half, half],
                    s1.at[a, e, 4 + half], r1.at[a, e, 4 + half], first_peer(a, d),
                )
    sums = []
    for e in order:
        for a in (0, 1):
            for half in (0, 1):
                plain[a, e, half].wait_recv()
                joint[a, e, half].wait_recv()
            total = srcs[a][slot(a, 0, e)] + in_side[a, e, 0].astype(F32) + in_side[a, e, 1].astype(F32)
            if e:
                out2[a, e - 1] = total.astype(BF)
                second[a, e] = send(out2.at[a, e - 1], in2.at[a, e - 1], s2.at[a, e - 1], r2.at[a, e - 1], second_peer(a, e))
            else:
                sums.append(total)
    for a, dst in ((0, k_sum), (1, v_sum)):
        total = sums[a]
        for e in (1, 2, 3):
            second[a, e].wait_recv()
            total = total + in2[a, e - 1].astype(F32)
        dst[...] = total
    for copy in across:
        copy.wait()
    for copy in [*far.values(), *plain.values(), *joint.values(), *second.values()]:
        copy.wait_send()


def reduce(dq_early, dq_late, dk, dv):
    dma = pltpu.SemaphoreType.DMA
    return pl.pallas_call(
        reduce_kernel,
        out_shape=(
            pltpu.VMEM((2, H * B, D), BF),
            pltpu.VMEM((2, D, B), F32),
            pltpu.VMEM((2, D, B), F32),
        ),
        in_specs=[VM] * 4,
        out_specs=(VM,) * 3,
        scratch_shapes=[
            pltpu.VMEM((2, PLANE, 2, D, B), BF),
            pltpu.VMEM((2, 4, 2, D, B), BF),
            pltpu.VMEM((2, 4, 2, D, B), BF),
            pltpu.VMEM((2, 4, 2, 2, D, B), BF),
            pltpu.VMEM((2, 3, 2, D, B), BF),
            pltpu.VMEM((2, 3, 2, D, B), BF),
            dma((2, 4, 6)), dma((2, 4, 6)), dma((2, 3)), dma((2, 3)), dma((2,)), dma((2,)),
        ],
        compiler_params=pltpu.CompilerParams(
            collective_id=1, has_side_effects=True, vmem_limit_bytes=VMEM_LIMIT
        ),
        name="reduce_rows",
    )(dq_early, dq_late, dk.reshape(PLANE, 2, D, B), dv.reshape(PLANE, 2, D, B))


def finish_kernel(dq_own, back, k_sum, v_sum, query_ref, key_ref, value_ref):
    scale = jnp.float32(D**-0.5)
    for blk in (0, 1):
        rows = slice(blk * B, (blk + 1) * B)
        for h in range(H):
            cols = slice(h * D, (h + 1) * D)
            query_ref[rows, cols] = (scale * (dq_own[blk, cols, :] + back[blk, cols, :].astype(F32))).astype(BF)
        key_ref[rows, :] = (scale * k_sum[blk]).T.astype(BF)
        value_ref[rows, :] = v_sum[blk].T.astype(BF)


def finish(*arrays):
    grad = jax.ShapeDtypeStruct((T, D), BF)
    return pl.pallas_call(
        finish_kernel,
        out_shape=(jax.ShapeDtypeStruct((T, H * D), BF), grad, grad),
        in_specs=[VM] * 4,
        out_specs=(VM,) * 3,
        compiler_params=pltpu.CompilerParams(vmem_limit_bytes=VMEM_LIMIT),
        name="finish",
    )(*arrays)


def local(queries, keys, values, outputs, out_grad, lse, block_order, doc_lengths):
    swap = [(i, i ^ 4) for i in range(2 * PLANE)]
    ka, va, rows, tail, stats, qt, gt, lc, dc, dk, dv = gather(keys, values, queries, out_grad, outputs, lse)
    pair_tail = lax.ppermute(tail, "ctx", swap)
    k = ka.reshape(2 * PLANE, B, D)
    v = va.reshape(2 * PLANE, B, D)
    dk, dv, dq_own, dq_early = attend(3, block_order, doc_lengths, k, v, rows, qt, gt, lc, dc, dk, dv)
    pair_rows = pair_tail.reshape(1, T, H * D)
    dk, dv, dq_late = attend(1, block_order, doc_lengths, k, v, pair_rows, stats, dk, dv)
    back, k_sum, v_sum = reduce(dq_early, dq_late, dk, dv)
    return finish(dq_own, back, k_sum, v_sum)


def solution(mesh):
    rows = P(("dp", "ctx"), None)
    return jax.shard_map(
        local,
        mesh=mesh,
        in_specs=(rows, rows, rows, rows, rows, P(None, ("dp", "ctx")), P("dp"), P("dp")),
        out_specs=(rows, rows, rows),
        check_vma=False,
    )
```

```python
import functools
import math

import jax
import jax.numpy as jnp
from jax import lax
from jax.experimental import pallas as pl
from jax.experimental.pallas import tpu as pltpu
from jax.sharding import PartitionSpec as P

BF = jnp.bfloat16
F32 = jnp.float32
I32 = jnp.int32
MESH = pl.DeviceIdType.MESH
VM = pl.BlockSpec(memory_space=pltpu.VMEM)
SM = pl.BlockSpec(memory_space=pltpu.SMEM)
ANY = pl.BlockSpec(memory_space=pl.ANY)

RING = 4
PLANE = RING * RING
T = 256
B = 128
H = 8
D = 128
VMEM_LIMIT = 32 * 2**20
LOG2E = math.log2(math.e)


def dot(a, b, ca, cb):
    return lax.dot_general(a, b, (((ca,), (cb,)), ((), ())), preferred_element_type=F32)


def stay(array):
    return pltpu.with_memory_space_constraint(array, pltpu.HBM)


def coords():
    me = lax.axis_index("ctx")
    return me // 8, (me // 4) % 2, me % 4


def ident(z, y, x):
    return {"ctx": z * 8 + y * 4 + x}


def step_of(v, d):
    return lax.rem(v + d, RING)


def greet_signal(z, y, x):
    barrier = pltpu.get_barrier_semaphore()
    others = [ident(z, y, step_of(x, d)) for d in (1, 2, 3)]
    others += [ident(step_of(z, d), y, x) for d in (1, 2, 3)]
    others.append(ident(z, 1 - y, x))
    for other in others:
        pl.semaphore_signal(barrier, inc=1, device_id=other, device_id_type=MESH)


def greet_wait():
    pl.semaphore_wait(pltpu.get_barrier_semaphore(), 7)


def pieces(whole):
    hi = whole.astype(BF)
    left = whole - hi.astype(F32)
    mid = left.astype(BF)
    return hi, mid, (left - mid.astype(F32)).astype(BF)


def widen(stats, side, blk, lc, dc, to):
    which = lax.broadcasted_iota(I32, (6 * H, D), 0) % (2 * H)
    parts = [stats[side, :, i * T + blk * B : i * T + (blk + 1) * B] for i in range(3)]
    parts = jnp.concatenate(parts, axis=0)
    for h in range(2 * H):
        select = jnp.where(which == h, 1.0, 0.0).astype(BF)
        (lc, dc)[h // H][to, h % H * D : (h % H + 1) * D, :] = dot(parts, select, 0, 0)


def turn(rows, blk, qt, gt):
    for dst, first in ((qt, 0), (gt, B)):
        for h in range(H):
            cols = slice(h * D, (h + 1) * D)
            dst[blk, :, cols] = rows[blk, first : first + B, cols].T


def gather_kernel(
    k_ref, v_ref, q_ref, g_ref, o_ref, lse_ref, ka, va, rows, tail, stats, qt, gt, lc, dc, dk, dv,
    outs, lses, own_sem, s1, r1, s2, r2, s3, r3, ps, pr,
):
    z, y, x = coords()
    here = z * RING + x
    pair = ident(z, 1 - y, x)
    greet_signal(z, y, x)
    copies = []

    def keep(src, dst):
        copy = pltpu.make_async_copy(src, dst, own_sem.at[len(copies)])
        copy.start()
        copies.append(copy)

    first_rows, last_rows = pl.ds(0, B), pl.ds(B, B)
    keep(g_ref.at[first_rows], rows.at[0, last_rows])
    keep(g_ref.at[last_rows], rows.at[1, last_rows])
    keep(o_ref, outs)
    keep(lse_ref, lses)
    keep(q_ref.at[first_rows], rows.at[0, first_rows])
    keep(q_ref.at[last_rows], rows.at[1, first_rows])
    keep(q_ref.at[last_rows], tail.at[first_rows])
    keep(g_ref.at[last_rows], tail.at[last_rows])
    keep(k_ref, ka.at[here])
    keep(v_ref, va.at[here])
    greet_wait()

    def send(src, dst, ssem, rsem, to):
        copy = pltpu.make_async_remote_copy(
            src_ref=src, dst_ref=dst, send_sem=ssem, recv_sem=rsem, device_id=to, device_id_type=MESH
        )
        copy.start()
        return copy

    srcs, alls = (k_ref, v_ref), (ka, va)

    def first_peer(a, d):
        return ident(z, y, step_of(x, d)) if a == 0 else ident(step_of(z, d), y, x)

    def second_peer(a, d):
        return first_peer(1 - a, d)

    def slot_from(a, s, t=0):
        if a == 0:
            return step_of(z, RING - t) * RING + step_of(x, RING - s)
        return step_of(z, RING - s) * RING + step_of(x, RING - t)

    first, second, third = {}, {}, {}

    def spread(a, s):
        src = srcs[a] if s == 0 else alls[a].at[slot_from(a, s)]
        dst = alls[a].at[here if s == 0 else slot_from(a, s)]
        for e in (1, 3, 2) if s == 2 else (1, 3):
            second[a, s, e] = send(src, dst, s2.at[a, s, e - 1], r2.at[a, s, e - 1], second_peer(a, e))

    for d in (1, 3, 2):
        for a in (0, 1):
            first[a, d] = send(srcs[a], alls[a].at[here], s1.at[a, d - 1], r1.at[a, d - 1], first_peer(a, d))
    for a in (0, 1):
        spread(a, 0)
    across = [
        send(q_ref.at[first_rows], rows.at[2, first_rows], ps.at[0], pr.at[0], pair),
        send(g_ref.at[first_rows], rows.at[2, last_rows], ps.at[1], pr.at[1], pair),
    ]

    for copy in copies[:4]:
        copy.wait()
    ones = jnp.ones((8, D), BF)
    deltas = []
    for h in range(H):
        cols = slice(h * D, (h + 1) * D)
        grad = jnp.concatenate([rows[0, B:, cols], rows[1, B:, cols]], axis=0)
        prod = grad.astype(F32) * outs[:, cols].astype(F32)
        hi = prod.astype(BF)
        lo = (prod - hi.astype(F32)).astype(BF)
        deltas.append((dot(ones, hi, 1, 1) + dot(ones, lo, 1, 1))[0:1, :])
    whole = jnp.concatenate([jnp.minimum(lses[...], 1e30) * jnp.float32(LOG2E)] + deltas, axis=0)
    for i, piece in enumerate(pieces(whole)):
        stats[0, :, i * T : (i + 1) * T] = piece
    stats[0, :, 3 * T :] = jnp.zeros((2 * H, T), BF)
    across.append(send(stats.at[0], stats.at[1], ps.at[2], pr.at[2], pair))

    def forward(s):
        for a in (0, 1):
            first[a, s].wait_recv()
            spread(a, s)

    forward(1)
    forward(3)
    forward(2)
    dk[...] = jnp.zeros_like(dk)
    dv[...] = jnp.zeros_like(dv)
    for copy in copies[4:]:
        copy.wait()
    for blk in (0, 1):
        widen(stats, 0, blk, lc, dc, blk)
        turn(rows, blk, qt, gt)

    def relay(s):
        for e, half in ((1, 0), (3, 1)):
            for a in (0, 1):
                second[a, s, e].wait_recv()
                part = alls[a].at[slot_from(a, s, e), pl.ds(half * B, B)]
                third[a, s, half] = send(part, part, s3.at[a, s, half], r3.at[a, s, half], second_peer(a, e))

    relay(0)
    relay(1)
    relay(3)
    for copy in across:
        copy.wait_recv()
    turn(rows, 2, qt, gt)
    widen(stats, 1, 0, lc, dc, 2)
    for a in (0, 1):
        for e in (1, 3, 2):
            second[a, 2, e].wait_recv()
    for copy in third.values():
        copy.wait_recv()
    for copy in list(first.values()) + list(second.values()) + list(third.values()) + across:
        copy.wait_send()


def gather(*arrays):
    dma = pltpu.SemaphoreType.DMA
    terms = pltpu.VMEM((3, H * B, D), F32)
    turned = pltpu.VMEM((3, D, H * B), BF)
    sums = pltpu.VMEM((2 * PLANE, D, B), F32)
    outs = (
        pltpu.VMEM((PLANE, T, D), BF),
        pltpu.VMEM((PLANE, T, D), BF),
        pltpu.VMEM((3, T, H * D), BF),
        pltpu.VMEM((T, H * D), BF),
        pltpu.VMEM((2, 2 * H, H * D), BF),
        turned, turned, terms, terms, sums, sums,
    )
    return pl.pallas_call(
        gather_kernel,
        out_shape=outs,
        in_specs=[ANY] * len(arrays),
        out_specs=(VM,) * len(outs),
        scratch_shapes=[
            pltpu.VMEM((T, H * D), BF),
            pltpu.VMEM((H, T), F32),
            dma((10,)), dma((2, 3)), dma((2, 3)), dma((2, 4, 3)), dma((2, 4, 3)),
            dma((2, 4, 2)), dma((2, 4, 2)), dma((3,)), dma((3,)),
        ],
        compiler_params=pltpu.CompilerParams(
            collective_id=0, has_side_effects=True, vmem_limit_bytes=VMEM_LIMIT
        ),
        name="gather_rows",
    )(*[stay(t) for t in arrays])


KEYS = 36
NEVER = 1 << 20


def attend_kernel(count, order, lens, *refs):
    early = count == 3
    if early:
        k_ref, v_ref, rows, qt, gt, lc, dc, _, _, dk, dv, dqa, dq_out = refs[:13]
        slots, places, qfrom, qbase, qlast, pbuf, dbuf = refs[13:]
    else:
        k_ref, v_ref, rows, stats, _, _, dk, dv, dq_out = refs[:9]
        slots, places, qfrom, qbase, qlast, pbuf, dbuf, qt, gt, lc, dc, dqa = refs[9:]
    me = lax.axis_index("ctx")
    plane = (me // 4) % 2
    mate = me + 4 - 8 * plane
    blocks = range(count)

    ats = [order[i] for i in ((me * 2, me * 2 + 1, mate * 2) if early else (mate * 2 + 1,))]
    row = lax.broadcasted_iota(I32, (B, D), 0)
    lows = [jnp.int32(0) for _ in blocks]
    lasts = [jnp.int32(0) for _ in blocks]
    begins = [jnp.zeros_like(row) for _ in blocks]
    end = jnp.int32(0)
    for d in range(lens.shape[0]):
        end = end + lens[d]
        for blk in blocks:
            lows[blk] = jnp.where(end <= ats[blk] * B, end, lows[blk])
            lasts[blk] = jnp.where(end <= ats[blk] * B + B - 1, end, lasts[blk])
            begins[blk] = jnp.where(end <= ats[blk] * B + row, end, begins[blk])
    lows = [low // B for low in lows]
    for blk in blocks:
        qfrom[blk] = begins[blk]
        qbase[blk] = ats[blk] * B
        qlast[blk] = lasts[blk]

    def list_keys(i, counts):
        counts = list(counts)
        for j in range(8):
            slot = i * 8 + j
            p = order[i * 16 + plane * 8 + j]
            for blk in blocks:
                slots[blk * KEYS + counts[blk]] = slot
                places[blk * KEYS + counts[blk]] = p * B
                needed = (p >= lows[blk]) & (p <= ats[blk])
                counts[blk] = counts[blk] + needed.astype(I32)
        return tuple(counts)

    counts = lax.fori_loop(0, 4, list_keys, tuple(jnp.int32(0) for _ in blocks))
    for blk in blocks:
        slots[blk * KEYS + counts[blk]] = 0
        places[blk * KEYS + counts[blk]] = NEVER
    items = [(n + 1) // 2 for n in counts]
    total = sum(items[1:], items[0])

    dqa[...] = jnp.zeros_like(dqa)
    if not early:
        widen(stats, 1, 1, lc, dc, 0)
        turn(rows, 0, qt, gt)
    scale = jnp.float32(D**-0.5 * LOG2E)
    across = lax.broadcasted_iota(I32, (1, B), 1)

    def load(n):
        at, which, past = 2 * n, jnp.int32(0), jnp.int32(0)
        for blk in blocks[:-1]:
            past = past + items[blk]
            later = n >= past
            which = which + later.astype(I32)
            at = at + jnp.where(later, KEYS - 2 * items[blk], 0)
        a, b = slots[at], slots[at + 1]
        kk = jnp.concatenate([k_ref[a], k_ref[b]], axis=0)
        vv = jnp.concatenate([v_ref[a], v_ref[b]], axis=0)
        return which, a, b, kk, vv, places[at], places[at + 1]

    def scores(item, par, masked=True):
        blk, _, _, kk, vv, place_a, place_b = item
        key_pos = jnp.concatenate([place_a + across, place_b + across], axis=1)
        here = qbase[blk] + row
        here = jnp.concatenate([here, here], axis=1)
        begin = qfrom[blk]
        begin = jnp.concatenate([begin, begin], axis=1)
        allowed = (key_pos <= here) & (key_pos >= begin)
        allowed = jnp.concatenate([allowed, allowed], axis=0)
        for two in range(4):
            cols = slice(two * 256, (two + 1) * 256)
            heads = [slice((2 * two + i) * D, (2 * two + i + 1) * D) for i in (0, 1)]
            score = dot(jnp.concatenate([rows[blk, :B, c] for c in heads], axis=0), kk, 1, 1)
            dprob = dot(jnp.concatenate([rows[blk, B:, c] for c in heads], axis=0), vv, 1, 1)
            less = lc[blk, cols, :]
            delta = dc[blk, cols, :]
            prob = jnp.exp2(score * scale - jnp.concatenate([less, less], axis=1))
            if masked:
                prob = jnp.where(allowed, prob, 0.0)
            pbuf[par, cols, :] = prob.astype(BF)
            dbuf[par, cols, :] = (prob * (dprob - jnp.concatenate([delta, delta], axis=1))).astype(BF)

    def grads(item, par):
        blk, a, b, kk = item[:4]
        dqa[blk] += jnp.dot(dbuf[par], kk, preferred_element_type=F32)
        dv_term = jnp.dot(gt[blk], pbuf[par], preferred_element_type=F32)
        dk_term = jnp.dot(qt[blk], dbuf[par], preferred_element_type=F32)
        dk[a] += dk_term[:, :B]
        dk[b] += dk_term[:, B:]
        dv[a] += dv_term[:, :B]
        dv[b] += dv_term[:, B:]

    def two(i, c):
        now = [load(2 * i), load(2 * i + 1)]
        open_ = None
        for blk, _, _, _, _, place_a, place_b in now:
            low = jnp.minimum(place_a, place_b) >= qlast[blk]
            high = jnp.maximum(place_a, place_b) < qbase[blk]
            open_ = low & high if open_ is None else open_ & low & high

        def run(masked):
            for par in (0, 1):
                scores(now[par], par, masked)
            for par in (0, 1):
                grads(now[par], par)

        pl.when(open_)(lambda: run(False))
        pl.when(jnp.logical_not(open_))(lambda: run(True))
        return c

    lax.fori_loop(0, total // 2, two, 0)

    @pl.when(total % 2 == 1)
    def _():
        last = load(total - 1)
        scores(last, 0)
        grads(last, 0)

    dq_out[...] = dqa[count - 1].astype(BF)


def attend(count, order, lens, *arrays):
    sums = pltpu.VMEM((2 * PLANE, D, B), F32)
    terms = pltpu.VMEM((count, H * B, D), F32)
    turned = pltpu.VMEM((count, D, H * B), BF)
    part = pltpu.VMEM((H * B, D), BF)
    scratch = [
        pltpu.SMEM((count * KEYS,), I32),
        pltpu.SMEM((count * KEYS,), I32),
        pltpu.VMEM((count, B, D), I32),
        pltpu.SMEM((count,), I32),
        pltpu.SMEM((count,), I32),
        pltpu.VMEM((2, H * B, 2 * B), BF),
        pltpu.VMEM((2, H * B, 2 * B), BF),
    ]
    if count == 3:
        outs = (sums, sums, terms, part)
    else:
        scratch += [turned, turned, terms, terms, terms]
        outs = (sums, sums, part)
    return pl.pallas_call(
        functools.partial(attend_kernel, count),
        out_shape=outs,
        in_specs=[SM] * 2 + [VM] * len(arrays),
        out_specs=(VM,) * len(outs),
        scratch_shapes=scratch,
        input_output_aliases={len(arrays): 0, len(arrays) + 1: 1},
        compiler_params=pltpu.CompilerParams(vmem_limit_bytes=VMEM_LIMIT),
        name="attend_early" if count == 3 else "attend_late",
    )(stay(order), stay(lens), *arrays)


def reduce_kernel(dq_early, dq_late, dk_ref, dv_ref, back, k_sum, v_sum, out1, in1, out_joint, in_side, out2, in2, s1, r1, s2, r2, ps, pr):
    z, y, x = coords()
    greet_signal(z, y, x)
    srcs = (dk_ref, dv_ref)
    for a in (0, 1):
        out1[a] = srcs[a][...].astype(BF)
    greet_wait()

    def send(src, dst, ssem, rsem, to):
        copy = pltpu.make_async_remote_copy(
            src_ref=src, dst_ref=dst, send_sem=ssem, recv_sem=rsem, device_id=to, device_id_type=MESH
        )
        copy.start()
        return copy

    def first_peer(a, d):
        return ident(step_of(z, d), y, x) if a == 0 else ident(z, y, step_of(x, d))

    def second_peer(a, e):
        return first_peer(1 - a, e)

    def slot(a, d, e):
        if a == 0:
            return step_of(z, d) * RING + step_of(x, e)
        return step_of(z, e) * RING + step_of(x, d)

    order, sides = (2, 1, 3, 0), ((1, 0), (3, 1))
    far, plain, joint, second = {}, {}, {}, {}
    for e in order:
        for a in (0, 1):
            for d, half in sides:
                far[a, e, half] = send(
                    out1.at[a, slot(a, 2, e), half], in1.at[a, e, half], s1.at[a, e, half], r1.at[a, e, half],
                    first_peer(a, d),
                )
    across = [
        send(src, back.at[blk], ps.at[blk], pr.at[blk], ident(z, 1 - y, x))
        for blk, src in enumerate((dq_early, dq_late))
    ]
    for e in order:
        for a in (0, 1):
            for d, half in sides:
                plain[a, e, half] = send(
                    out1.at[a, slot(a, d, e), 1 - half], in_side.at[a, e, half, 1 - half],
                    s1.at[a, e, 2 + half], r1.at[a, e, 2 + half], first_peer(a, d),
                )
        for a in (0, 1):
            for d, half in sides:
                far[a, e, half].wait_recv()
                both = srcs[a][slot(a, d, e), half] + in1[a, e, half].astype(F32)
                out_joint[a, e, half] = both.astype(BF)
                joint[a, e, half] = send(
                    out_joint.at[a, e, half], in_side.at[a, e, half, half],
                    s1.at[a, e, 4 + half], r1.at[a, e, 4 + half], first_peer(a, d),
                )
    sums = []
    for e in order:
        for a in (0, 1):
            for half in (0, 1):
                plain[a, e, half].wait_recv()
                joint[a, e, half].wait_recv()
            total = srcs[a][slot(a, 0, e)] + in_side[a, e, 0].astype(F32) + in_side[a, e, 1].astype(F32)
            if e:
                out2[a, e - 1] = total.astype(BF)
                second[a, e] = send(out2.at[a, e - 1], in2.at[a, e - 1], s2.at[a, e - 1], r2.at[a, e - 1], second_peer(a, e))
            else:
                sums.append(total)
    for a, dst in ((0, k_sum), (1, v_sum)):
        total = sums[a]
        for e in (1, 2, 3):
            second[a, e].wait_recv()
            total = total + in2[a, e - 1].astype(F32)
        dst[...] = total
    for copy in across:
        copy.wait()
    for copy in [*far.values(), *plain.values(), *joint.values(), *second.values()]:
        copy.wait_send()


def reduce(dq_early, dq_late, dk, dv):
    dma = pltpu.SemaphoreType.DMA
    return pl.pallas_call(
        reduce_kernel,
        out_shape=(
            pltpu.VMEM((2, H * B, D), BF),
            pltpu.VMEM((2, D, B), F32),
            pltpu.VMEM((2, D, B), F32),
        ),
        in_specs=[VM] * 4,
        out_specs=(VM,) * 3,
        scratch_shapes=[
            pltpu.VMEM((2, PLANE, 2, D, B), BF),
            pltpu.VMEM((2, 4, 2, D, B), BF),
            pltpu.VMEM((2, 4, 2, D, B), BF),
            pltpu.VMEM((2, 4, 2, 2, D, B), BF),
            pltpu.VMEM((2, 3, 2, D, B), BF),
            pltpu.VMEM((2, 3, 2, D, B), BF),
            dma((2, 4, 6)), dma((2, 4, 6)), dma((2, 3)), dma((2, 3)), dma((2,)), dma((2,)),
        ],
        compiler_params=pltpu.CompilerParams(
            collective_id=1, has_side_effects=True, vmem_limit_bytes=VMEM_LIMIT
        ),
        name="reduce_rows",
    )(dq_early, dq_late, dk.reshape(PLANE, 2, D, B), dv.reshape(PLANE, 2, D, B))


def finish_kernel(dq_own, back, k_sum, v_sum, query_ref, key_ref, value_ref):
    scale = jnp.float32(D**-0.5)
    for blk in (0, 1):
        rows = slice(blk * B, (blk + 1) * B)
        for h in range(H):
            cols = slice(h * D, (h + 1) * D)
            query_ref[rows, cols] = (scale * (dq_own[blk, cols, :] + back[blk, cols, :].astype(F32))).astype(BF)
        key_ref[rows, :] = (scale * k_sum[blk]).T.astype(BF)
        value_ref[rows, :] = v_sum[blk].T.astype(BF)


def finish(*arrays):
    grad = jax.ShapeDtypeStruct((T, D), BF)
    return pl.pallas_call(
        finish_kernel,
        out_shape=(jax.ShapeDtypeStruct((T, H * D), BF), grad, grad),
        in_specs=[VM] * 4,
        out_specs=(VM,) * 3,
        compiler_params=pltpu.CompilerParams(vmem_limit_bytes=VMEM_LIMIT),
        name="finish",
    )(*arrays)


def local(queries, keys, values, outputs, out_grad, lse, block_order, doc_lengths):
    swap = [(i, i ^ 4) for i in range(2 * PLANE)]
    ka, va, rows, tail, stats, qt, gt, lc, dc, dk, dv = gather(keys, values, queries, out_grad, outputs, lse)
    pair_tail = lax.ppermute(tail, "ctx", swap)
    k = ka.reshape(2 * PLANE, B, D)
    v = va.reshape(2 * PLANE, B, D)
    dk, dv, dq_own, dq_early = attend(3, block_order, doc_lengths, k, v, rows, qt, gt, lc, dc, dk, dv)
    pair_rows = pair_tail.reshape(1, T, H * D)
    dk, dv, dq_late = attend(1, block_order, doc_lengths, k, v, pair_rows, stats, dk, dv)
    back, k_sum, v_sum = reduce(dq_early, dq_late, dk, dv)
    return finish(dq_own, back, k_sum, v_sum)


def solution(mesh):
    rows = P(("dp", "ctx"), None)
    return jax.shard_map(
        local,
        mesh=mesh,
        in_specs=(rows, rows, rows, rows, rows, P(None, ("dp", "ctx")), P("dp"), P("dp")),
        out_specs=(rows, rows, rows),
        check_vma=False,
    )
```

```python
import functools
import math

import jax
import jax.numpy as jnp
from jax import lax
from jax.experimental import pallas as pl
from jax.experimental.pallas import tpu as pltpu
from jax.sharding import PartitionSpec as P

BF = jnp.bfloat16
F32 = jnp.float32
I32 = jnp.int32
MESH = pl.DeviceIdType.MESH
VM = pl.BlockSpec(memory_space=pltpu.VMEM)
SM = pl.BlockSpec(memory_space=pltpu.SMEM)
ANY = pl.BlockSpec(memory_space=pl.ANY)

RING = 4
PLANE = RING * RING
T = 256
B = 128
H = 8
D = 128
VMEM_LIMIT = 32 * 2**20
LOG2E = math.log2(math.e)


def dot(a, b, ca, cb):
    return lax.dot_general(a, b, (((ca,), (cb,)), ((), ())), preferred_element_type=F32)


def stay(array):
    return pltpu.with_memory_space_constraint(array, pltpu.HBM)


def coords():
    me = lax.axis_index("ctx")
    return me // 8, (me // 4) % 2, me % 4


def ident(z, y, x):
    return {"ctx": z * 8 + y * 4 + x}


def step_of(v, d):
    return lax.rem(v + d, RING)


def greet_signal(z, y, x):
    barrier = pltpu.get_barrier_semaphore()
    others = [ident(z, y, step_of(x, d)) for d in (1, 2, 3)]
    others += [ident(step_of(z, d), y, x) for d in (1, 2, 3)]
    others.append(ident(z, 1 - y, x))
    for other in others:
        pl.semaphore_signal(barrier, inc=1, device_id=other, device_id_type=MESH)


def greet_wait():
    pl.semaphore_wait(pltpu.get_barrier_semaphore(), 7)


def pieces(whole):
    hi = whole.astype(BF)
    left = whole - hi.astype(F32)
    mid = left.astype(BF)
    return hi, mid, (left - mid.astype(F32)).astype(BF)


def widen(stats, side, blk, lc, dc, to):
    which = lax.broadcasted_iota(I32, (6 * H, D), 0) % (2 * H)
    parts = [stats[side, :, i * T + blk * B : i * T + (blk + 1) * B] for i in range(3)]
    parts = jnp.concatenate(parts, axis=0)
    for h in range(2 * H):
        select = jnp.where(which == h, 1.0, 0.0).astype(BF)
        (lc, dc)[h // H][to, h % H * D : (h % H + 1) * D, :] = dot(parts, select, 0, 0)


def turn(rows, blk, qt, gt):
    for dst, first in ((qt, 0), (gt, B)):
        for h in range(H):
            cols = slice(h * D, (h + 1) * D)
            dst[blk, :, cols] = rows[blk, first : first + B, cols].T


def gather_kernel(
    k_ref, v_ref, q_ref, g_ref, o_ref, lse_ref, ka, va, rows, tail, stats, qt, gt, lc, dc, dk, dv,
    outs, lses, own_sem, s1, r1, s2, r2, s3, r3, ps, pr,
):
    z, y, x = coords()
    here = z * RING + x
    pair = ident(z, 1 - y, x)
    greet_signal(z, y, x)
    copies = []

    def keep(src, dst):
        copy = pltpu.make_async_copy(src, dst, own_sem.at[len(copies)])
        copy.start()
        copies.append(copy)

    first_rows, last_rows = pl.ds(0, B), pl.ds(B, B)
    keep(g_ref.at[first_rows], rows.at[0, last_rows])
    keep(g_ref.at[last_rows], rows.at[1, last_rows])
    keep(o_ref, outs)
    keep(lse_ref, lses)
    keep(q_ref.at[first_rows], rows.at[0, first_rows])
    keep(q_ref.at[last_rows], rows.at[1, first_rows])
    keep(q_ref.at[last_rows], tail.at[first_rows])
    keep(g_ref.at[last_rows], tail.at[last_rows])
    keep(k_ref, ka.at[here])
    keep(v_ref, va.at[here])
    greet_wait()

    def send(src, dst, ssem, rsem, to):
        copy = pltpu.make_async_remote_copy(
            src_ref=src, dst_ref=dst, send_sem=ssem, recv_sem=rsem, device_id=to, device_id_type=MESH
        )
        copy.start()
        return copy

    across = [
        send(q_ref.at[first_rows], rows.at[2, first_rows], ps.at[0], pr.at[0], pair),
        send(g_ref.at[first_rows], rows.at[2, last_rows], ps.at[1], pr.at[1], pair),
    ]

    srcs, alls = (k_ref, v_ref), (ka, va)

    def first_peer(a, d):
        return ident(z, y, step_of(x, d)) if a == 0 else ident(step_of(z, d), y, x)

    def second_peer(a, d):
        return first_peer(1 - a, d)

    def slot_from(a, s, t=0):
        if a == 0:
            return step_of(z, RING - t) * RING + step_of(x, RING - s)
        return step_of(z, RING - s) * RING + step_of(x, RING - t)

    first, second, third = {}, {}, {}

    def spread(a, s):
        src = srcs[a] if s == 0 else alls[a].at[slot_from(a, s)]
        dst = alls[a].at[here if s == 0 else slot_from(a, s)]
        for e in (1, 3, 2) if s == 2 else (1, 3):
            second[a, s, e] = send(src, dst, s2.at[a, s, e - 1], r2.at[a, s, e - 1], second_peer(a, e))

    for d in (1, 3, 2):
        for a in (0, 1):
            first[a, d] = send(srcs[a], alls[a].at[here], s1.at[a, d - 1], r1.at[a, d - 1], first_peer(a, d))
    for a in (0, 1):
        spread(a, 0)

    for copy in copies[:4]:
        copy.wait()
    ones = jnp.ones((8, D), BF)
    deltas = []
    for h in range(H):
        cols = slice(h * D, (h + 1) * D)
        grad = jnp.concatenate([rows[0, B:, cols], rows[1, B:, cols]], axis=0)
        prod = grad.astype(F32) * outs[:, cols].astype(F32)
        hi = prod.astype(BF)
        lo = (prod - hi.astype(F32)).astype(BF)
        deltas.append((dot(ones, hi, 1, 1) + dot(ones, lo, 1, 1))[0:1, :])
    whole = jnp.concatenate([jnp.minimum(lses[...], 1e30) * jnp.float32(LOG2E)] + deltas, axis=0)
    for i, piece in enumerate(pieces(whole)):
        stats[0, :, i * T : (i + 1) * T] = piece
    stats[0, :, 3 * T :] = jnp.zeros((2 * H, T), BF)
    across.append(send(stats.at[0], stats.at[1], ps.at[2], pr.at[2], pair))

    def forward(s):
        for a in (0, 1):
            first[a, s].wait_recv()
            spread(a, s)

    forward(1)
    forward(3)
    forward(2)
    dk[...] = jnp.zeros_like(dk)
    dv[...] = jnp.zeros_like(dv)
    for copy in copies[4:]:
        copy.wait()
    for blk in (0, 1):
        widen(stats, 0, blk, lc, dc, blk)
        turn(rows, blk, qt, gt)

    def relay(s):
        for e, half in ((1, 0), (3, 1)):
            for a in (0, 1):
                second[a, s, e].wait_recv()
                part = alls[a].at[slot_from(a, s, e), pl.ds(half * B, B)]
                third[a, s, half] = send(part, part, s3.at[a, s, half], r3.at[a, s, half], second_peer(a, e))

    relay(0)
    relay(1)
    relay(3)
    for copy in across:
        copy.wait_recv()
    turn(rows, 2, qt, gt)
    widen(stats, 1, 0, lc, dc, 2)
    for a in (0, 1):
        for e in (1, 3, 2):
            second[a, 2, e].wait_recv()
    for copy in third.values():
        copy.wait_recv()
    for copy in list(first.values()) + list(second.values()) + list(third.values()) + across:
        copy.wait_send()


def gather(*arrays):
    dma = pltpu.SemaphoreType.DMA
    terms = pltpu.VMEM((3, H * B, D), F32)
    turned = pltpu.VMEM((3, D, H * B), BF)
    sums = pltpu.VMEM((2 * PLANE, D, B), F32)
    outs = (
        pltpu.VMEM((PLANE, T, D), BF),
        pltpu.VMEM((PLANE, T, D), BF),
        pltpu.VMEM((3, T, H * D), BF),
        pltpu.VMEM((T, H * D), BF),
        pltpu.VMEM((2, 2 * H, H * D), BF),
        turned, turned, terms, terms, sums, sums,
    )
    return pl.pallas_call(
        gather_kernel,
        out_shape=outs,
        in_specs=[ANY] * len(arrays),
        out_specs=(VM,) * len(outs),
        scratch_shapes=[
            pltpu.VMEM((T, H * D), BF),
            pltpu.VMEM((H, T), F32),
            dma((10,)), dma((2, 3)), dma((2, 3)), dma((2, 4, 3)), dma((2, 4, 3)),
            dma((2, 4, 2)), dma((2, 4, 2)), dma((3,)), dma((3,)),
        ],
        compiler_params=pltpu.CompilerParams(
            collective_id=0, has_side_effects=True, vmem_limit_bytes=VMEM_LIMIT
        ),
        name="gather_rows",
    )(*[stay(t) for t in arrays])


KEYS = 36
NEVER = 1 << 20


def attend_kernel(count, order, lens, *refs):
    early = count == 3
    if early:
        k_ref, v_ref, rows, qt, gt, lc, dc, _, _, dk, dv, dqa, dq_out = refs[:13]
        slots, places, qfrom, qbase, pbuf, dbuf = refs[13:]
    else:
        k_ref, v_ref, rows, stats, _, _, dk, dv, dq_out = refs[:9]
        slots, places, qfrom, qbase, pbuf, dbuf, qt, gt, lc, dc, dqa = refs[9:]
    me = lax.axis_index("ctx")
    plane = (me // 4) % 2
    mate = me + 4 - 8 * plane
    blocks = range(count)

    ats = [order[i] for i in ((me * 2, me * 2 + 1, mate * 2) if early else (mate * 2 + 1,))]
    row = lax.broadcasted_iota(I32, (B, D), 0)
    lows = [jnp.int32(0) for _ in blocks]
    begins = [jnp.zeros_like(row) for _ in blocks]
    end = jnp.int32(0)
    for d in range(lens.shape[0]):
        end = end + lens[d]
        for blk in blocks:
            lows[blk] = jnp.where(end <= ats[blk] * B, end, lows[blk])
            begins[blk] = jnp.where(end <= ats[blk] * B + row, end, begins[blk])
    lows = [low // B for low in lows]
    for blk in blocks:
        qfrom[blk] = begins[blk]
        qbase[blk] = ats[blk] * B

    def list_keys(i, counts):
        counts = list(counts)
        for j in range(8):
            slot = i * 8 + j
            p = order[i * 16 + plane * 8 + j]
            for blk in blocks:
                slots[blk * KEYS + counts[blk]] = slot
                places[blk * KEYS + counts[blk]] = p * B
                needed = (p >= lows[blk]) & (p <= ats[blk])
                counts[blk] = counts[blk] + needed.astype(I32)
        return tuple(counts)

    counts = lax.fori_loop(0, 4, list_keys, tuple(jnp.int32(0) for _ in blocks))
    for blk in blocks:
        slots[blk * KEYS + counts[blk]] = 0
        places[blk * KEYS + counts[blk]] = NEVER
    items = [(n + 1) // 2 for n in counts]
    total = sum(items[1:], items[0])

    dqa[...] = jnp.zeros_like(dqa)
    if not early:
        widen(stats, 1, 1, lc, dc, 0)
        turn(rows, 0, qt, gt)
    scale = jnp.float32(D**-0.5 * LOG2E)
    across = lax.broadcasted_iota(I32, (1, B), 1)

    def load(n):
        at, which, past = 2 * n, jnp.int32(0), jnp.int32(0)
        for blk in blocks[:-1]:
            past = past + items[blk]
            later = n >= past
            which = which + later.astype(I32)
            at = at + jnp.where(later, KEYS - 2 * items[blk], 0)
        a, b = slots[at], slots[at + 1]
        kk = jnp.concatenate([k_ref[a], k_ref[b]], axis=0)
        vv = jnp.concatenate([v_ref[a], v_ref[b]], axis=0)
        return which, a, b, kk, vv, places[at], places[at + 1]

    def scores(item, par):
        blk, _, _, kk, vv, place_a, place_b = item
        key_pos = jnp.concatenate([place_a + across, place_b + across], axis=1)
        here = qbase[blk] + row
        here = jnp.concatenate([here, here], axis=1)
        begin = qfrom[blk]
        begin = jnp.concatenate([begin, begin], axis=1)
        allowed = (key_pos <= here) & (key_pos >= begin)
        allowed = jnp.concatenate([allowed, allowed], axis=0)
        for two in range(4):
            cols = slice(two * 256, (two + 1) * 256)
            heads = [slice((2 * two + i) * D, (2 * two + i + 1) * D) for i in (0, 1)]
            score = dot(jnp.concatenate([rows[blk, :B, c] for c in heads], axis=0), kk, 1, 1)
            dprob = dot(jnp.concatenate([rows[blk, B:, c] for c in heads], axis=0), vv, 1, 1)
            less = lc[blk, cols, :]
            delta = dc[blk, cols, :]
            prob = jnp.where(allowed, jnp.exp2(score * scale - jnp.concatenate([less, less], axis=1)), 0.0)
            pbuf[par, cols, :] = prob.astype(BF)
            dbuf[par, cols, :] = (prob * (dprob - jnp.concatenate([delta, delta], axis=1))).astype(BF)

    def grads(item, par):
        blk, a, b, kk = item[:4]
        dqa[blk] += jnp.dot(dbuf[par], kk, preferred_element_type=F32)
        dv_term = jnp.dot(gt[blk], pbuf[par], preferred_element_type=F32)
        dk_term = jnp.dot(qt[blk], dbuf[par], preferred_element_type=F32)
        dk[a] += dk_term[:, :B]
        dk[b] += dk_term[:, B:]
        dv[a] += dv_term[:, :B]
        dv[b] += dv_term[:, B:]

    def two(i, c):
        now = [load(2 * i), load(2 * i + 1)]
        for par in (0, 1):
            scores(now[par], par)
        for par in (0, 1):
            grads(now[par], par)
        return c

    lax.fori_loop(0, total // 2, two, 0)

    @pl.when(total % 2 == 1)
    def _():
        last = load(total - 1)
        scores(last, 0)
        grads(last, 0)

    dq_out[...] = dqa[count - 1].astype(BF)


def attend(count, order, lens, *arrays):
    sums = pltpu.VMEM((2 * PLANE, D, B), F32)
    terms = pltpu.VMEM((count, H * B, D), F32)
    turned = pltpu.VMEM((count, D, H * B), BF)
    part = pltpu.VMEM((H * B, D), BF)
    scratch = [
        pltpu.SMEM((count * KEYS,), I32),
        pltpu.SMEM((count * KEYS,), I32),
        pltpu.VMEM((count, B, D), I32),
        pltpu.SMEM((count,), I32),
        pltpu.VMEM((2, H * B, 2 * B), BF),
        pltpu.VMEM((2, H * B, 2 * B), BF),
    ]
    if count == 3:
        outs = (sums, sums, terms, part)
    else:
        scratch += [turned, turned, terms, terms, terms]
        outs = (sums, sums, part)
    return pl.pallas_call(
        functools.partial(attend_kernel, count),
        out_shape=outs,
        in_specs=[SM] * 2 + [VM] * len(arrays),
        out_specs=(VM,) * len(outs),
        scratch_shapes=scratch,
        input_output_aliases={len(arrays): 0, len(arrays) + 1: 1},
        compiler_params=pltpu.CompilerParams(vmem_limit_bytes=VMEM_LIMIT),
        name="attend_early" if count == 3 else "attend_late",
    )(stay(order), stay(lens), *arrays)


def reduce_kernel(dq_early, dq_late, dk_ref, dv_ref, back, k_sum, v_sum, out1, in1, out_joint, in_side, out2, in2, s1, r1, s2, r2, ps, pr):
    z, y, x = coords()
    greet_signal(z, y, x)
    srcs = (dk_ref, dv_ref)
    for a in (0, 1):
        out1[a] = srcs[a][...].astype(BF)
    greet_wait()

    def send(src, dst, ssem, rsem, to):
        copy = pltpu.make_async_remote_copy(
            src_ref=src, dst_ref=dst, send_sem=ssem, recv_sem=rsem, device_id=to, device_id_type=MESH
        )
        copy.start()
        return copy

    def first_peer(a, d):
        return ident(step_of(z, d), y, x) if a == 0 else ident(z, y, step_of(x, d))

    def second_peer(a, e):
        return first_peer(1 - a, e)

    def slot(a, d, e):
        if a == 0:
            return step_of(z, d) * RING + step_of(x, e)
        return step_of(z, e) * RING + step_of(x, d)

    order, sides = (2, 1, 3, 0), ((1, 0), (3, 1))
    far, plain, joint, second = {}, {}, {}, {}
    for e in order:
        for a in (0, 1):
            for d, half in sides:
                far[a, e, half] = send(
                    out1.at[a, slot(a, 2, e), half], in1.at[a, e, half], s1.at[a, e, half], r1.at[a, e, half],
                    first_peer(a, d),
                )
    across = [
        send(src, back.at[blk], ps.at[blk], pr.at[blk], ident(z, 1 - y, x))
        for blk, src in enumerate((dq_early, dq_late))
    ]
    for e in order:
        for a in (0, 1):
            for d, half in sides:
                plain[a, e, half] = send(
                    out1.at[a, slot(a, d, e), 1 - half], in_side.at[a, e, half, 1 - half],
                    s1.at[a, e, 2 + half], r1.at[a, e, 2 + half], first_peer(a, d),
                )
        for a in (0, 1):
            for d, half in sides:
                far[a, e, half].wait_recv()
                both = srcs[a][slot(a, d, e), half] + in1[a, e, half].astype(F32)
                out_joint[a, e, half] = both.astype(BF)
                joint[a, e, half] = send(
                    out_joint.at[a, e, half], in_side.at[a, e, half, half],
                    s1.at[a, e, 4 + half], r1.at[a, e, 4 + half], first_peer(a, d),
                )
    sums = []
    for e in order:
        for a in (0, 1):
            for half in (0, 1):
                plain[a, e, half].wait_recv()
                joint[a, e, half].wait_recv()
            total = srcs[a][slot(a, 0, e)] + in_side[a, e, 0].astype(F32) + in_side[a, e, 1].astype(F32)
            if e:
                out2[a, e - 1] = total.astype(BF)
                second[a, e] = send(out2.at[a, e - 1], in2.at[a, e - 1], s2.at[a, e - 1], r2.at[a, e - 1], second_peer(a, e))
            else:
                sums.append(total)
    for a, dst in ((0, k_sum), (1, v_sum)):
        total = sums[a]
        for e in (1, 2, 3):
            second[a, e].wait_recv()
            total = total + in2[a, e - 1].astype(F32)
        dst[...] = total
    for copy in across:
        copy.wait()
    for copy in [*far.values(), *plain.values(), *joint.values(), *second.values()]:
        copy.wait_send()


def reduce(dq_early, dq_late, dk, dv):
    dma = pltpu.SemaphoreType.DMA
    return pl.pallas_call(
        reduce_kernel,
        out_shape=(
            pltpu.VMEM((2, H * B, D), BF),
            pltpu.VMEM((2, D, B), F32),
            pltpu.VMEM((2, D, B), F32),
        ),
        in_specs=[VM] * 4,
        out_specs=(VM,) * 3,
        scratch_shapes=[
            pltpu.VMEM((2, PLANE, 2, D, B), BF),
            pltpu.VMEM((2, 4, 2, D, B), BF),
            pltpu.VMEM((2, 4, 2, D, B), BF),
            pltpu.VMEM((2, 4, 2, 2, D, B), BF),
            pltpu.VMEM((2, 3, 2, D, B), BF),
            pltpu.VMEM((2, 3, 2, D, B), BF),
            dma((2, 4, 6)), dma((2, 4, 6)), dma((2, 3)), dma((2, 3)), dma((2,)), dma((2,)),
        ],
        compiler_params=pltpu.CompilerParams(
            collective_id=1, has_side_effects=True, vmem_limit_bytes=VMEM_LIMIT
        ),
        name="reduce_rows",
    )(dq_early, dq_late, dk.reshape(PLANE, 2, D, B), dv.reshape(PLANE, 2, D, B))


def finish_kernel(dq_own, back, k_sum, v_sum, query_ref, key_ref, value_ref):
    scale = jnp.float32(D**-0.5)
    for blk in (0, 1):
        rows = slice(blk * B, (blk + 1) * B)
        for h in range(H):
            cols = slice(h * D, (h + 1) * D)
            query_ref[rows, cols] = (scale * (dq_own[blk, cols, :] + back[blk, cols, :].astype(F32))).astype(BF)
        key_ref[rows, :] = (scale * k_sum[blk]).T.astype(BF)
        value_ref[rows, :] = v_sum[blk].T.astype(BF)


def finish(*arrays):
    grad = jax.ShapeDtypeStruct((T, D), BF)
    return pl.pallas_call(
        finish_kernel,
        out_shape=(jax.ShapeDtypeStruct((T, H * D), BF), grad, grad),
        in_specs=[VM] * 4,
        out_specs=(VM,) * 3,
        compiler_params=pltpu.CompilerParams(vmem_limit_bytes=VMEM_LIMIT),
        name="finish",
    )(*arrays)


def local(queries, keys, values, outputs, out_grad, lse, block_order, doc_lengths):
    swap = [(i, i ^ 4) for i in range(2 * PLANE)]
    ka, va, rows, tail, stats, qt, gt, lc, dc, dk, dv = gather(keys, values, queries, out_grad, outputs, lse)
    pair_tail = lax.ppermute(tail, "ctx", swap)
    k = ka.reshape(2 * PLANE, B, D)
    v = va.reshape(2 * PLANE, B, D)
    dk, dv, dq_own, dq_early = attend(3, block_order, doc_lengths, k, v, rows, qt, gt, lc, dc, dk, dv)
    pair_rows = pair_tail.reshape(1, T, H * D)
    dk, dv, dq_late = attend(1, block_order, doc_lengths, k, v, pair_rows, stats, dk, dv)
    back, k_sum, v_sum = reduce(dq_early, dq_late, dk, dv)
    return finish(dq_own, back, k_sum, v_sum)


def solution(mesh):
    rows = P(("dp", "ctx"), None)
    return jax.shard_map(
        local,
        mesh=mesh,
        in_specs=(rows, rows, rows, rows, rows, P(None, ("dp", "ctx")), P("dp"), P("dp")),
        out_specs=(rows, rows, rows),
        check_vma=False,
    )
```
